512 devices in a mesh: mp: 8 (over y, core), tx: 4 (over z_hi), ty: 16 (over x, z_lo).
Axes of the slice: x: 4, y: 4, z: 16 (z_hi: 4, z_lo: 4; z = z_hi * 4 + z_lo), core: 2. Of those that a mesh axis runs over, the one named last changes fastest.
Arguments:
- models: float32 [8, 16, 256, 512], P('mp', None, 'ty', 'tx'), may hold values from -6 to 6
- direction: float32 [8, 16, 256, 512], P('mp', None, 'ty', 'tx'), may hold values from -6 to 6
- coupling: float32 [8], replicated, may hold values from 0.1 to 0.4
- tv_weight: float32 [8], replicated, may hold values from 0.5 to 2
Outputs:
- gradient: float32 [8, 16, 256, 512], P('mp', None, 'ty', 'tx')
- hessian_vector: float32 [8, 16, 256, 512], P('mp', None, 'ty', 'tx')
The draws below stay inside these ranges and needn't reach their ends.
All inputs are finite; a program needn't handle non-finite values.
Results may differ from the reference program's by a relative error of at most 0.0001.
Values sent between devices are 32-bit elements; how exact they have to be, the bound alone decides.
A program may use at most 64 MiB of HBM per device.

```python
import math
import jax
import jax.numpy as jnp
from jax import lax

NZ = 16
MODELS = 8
NX = 512
NY = 256


def block_levels(rng, extent, pieces, smallest, high):
    def one(dim, shards_of):
        heights = jax.random.uniform(jax.random.fold_in(jax.random.fold_in(rng, 6), dim), (shards_of,), jnp.float32, smallest / len(pieces), high / len(pieces))
        return jnp.repeat(jnp.exp(heights), extent[dim] // shards_of).reshape((-1,) + (1,) * (len(extent) - dim - 1))

    gain = one(*pieces[0])
    for cut in pieces[1:]:
        gain = gain * one(*cut)
    return gain


def scatter_about(stream_key, shape, spread, most, cuts=(), held_as=jnp.bfloat16):
    array = jax.random.normal(stream_key, shape, jnp.float32) * spread
    if len(cuts) > 0:
        array = block_levels(stream_key, shape, cuts, -0.22, 0.18) * array
    return jnp.clip(array, min=-most, max=most).astype(held_as)


def setup_inputs(seed: int = 0) -> dict:
    arg_keys = jax.random.split(jax.random.key(seed), 5)
    return {
        "models": scatter_about(arg_keys[0], (MODELS, NZ, NY, NX), 1.0, 6.0, ((0, 8), (2, 16), (3, 4)), jnp.float32),
        "direction": scatter_about(arg_keys[1], (MODELS, NZ, NY, NX), 1.0, 6.0, ((0, 8), (2, 16), (3, 4)), jnp.float32),
        "coupling": jnp.clip(jnp.exp(jax.random.uniform(arg_keys[2], (MODELS,), jnp.float32, math.log(0.1), math.log(0.4))), 0.1, 0.4),
        "tv_weight": jnp.clip(jnp.exp(jax.random.uniform(arg_keys[3], (MODELS,), jnp.float32, math.log(0.5), math.log(2.0))), 0.5, 2.0),
    }


EPS_SQ = 0.25
SYM_PAIRS = ((0, 0), (1, 1), (2, 2), (0, 1), (0, 2), (1, 2))

def forward_diffs(field):
    dx = jnp.concatenate([field[..., 1:] - field[..., :-1], jnp.zeros_like(field[..., :1])], -1)
    dy = jnp.concatenate([field[..., 1:, :] - field[..., :-1, :], jnp.zeros_like(field[..., :1, :])], -2)
    dz = jnp.concatenate([field[..., 1:, :, :] - field[..., :-1, :, :], jnp.zeros_like(field[..., :1, :, :])], -3)
    return jnp.stack([dx, dy, dz], axis=-4)

def adjoint(flux):
    fx = flux[..., 0, :, :, :]
    fy = flux[..., 1, :, :, :]
    fz = flux[..., 2, :, :, :]
    mx = jnp.concatenate([fx[..., :-1], jnp.zeros_like(fx[..., :1])], -1)
    my = jnp.concatenate([fy[..., :-1, :], jnp.zeros_like(fy[..., :1, :])], -2)
    mz = jnp.concatenate([fz[..., :-1, :, :], jnp.zeros_like(fz[..., :1, :, :])], -3)
    res = jnp.concatenate([jnp.zeros_like(fx[..., :1]), mx[..., :-1]], -1) - mx
    res = res + jnp.concatenate([jnp.zeros_like(fy[..., :1, :]), my[..., :-1, :]], -2) - my
    res = res + jnp.concatenate([jnp.zeros_like(fz[..., :1, :, :]), mz[..., :-1, :, :]], -3) - mz
    return res

def moments(grads, dirs, weights):
    wts = weights[:, None, None, None]
    rows = [lax.optimization_barrier(jnp.sum(wts * grads[:, i] * grads[:, j], 0)) for i, j in SYM_PAIRS]
    for i in range(3):
        for j in range(3):
            rows.append(lax.optimization_barrier(jnp.sum(wts * dirs[:, i] * grads[:, j], 0)))
    return jnp.stack(rows, 0)

def couple(moms, grad_own, dir_own):
    trace_m = moms[0] + moms[1] + moms[2]
    mat = [[moms[0], moms[3], moms[4]], [moms[3], moms[1], moms[5]], [moms[4], moms[5], moms[2]]]
    nat = [[moms[6 + 3 * i + j] for j in range(3)] for i in range(3)]
    trace_n = nat[0][0] + nat[1][1] + nat[2][2]
    g_parts = [grad_own[..., i, :, :, :] for i in range(3)]
    e_parts = [dir_own[..., i, :, :, :] for i in range(3)]
    cross_q = []
    cross_p = []
    for i in range(3):
        mg = mat[i][0] * g_parts[0] + mat[i][1] * g_parts[1] + mat[i][2] * g_parts[2]
        me = mat[i][0] * e_parts[0] + mat[i][1] * e_parts[1] + mat[i][2] * e_parts[2]
        ng = nat[i][0] * g_parts[0] + nat[i][1] * g_parts[1] + nat[i][2] * g_parts[2]
        cross_q.append(trace_m * g_parts[i] - mg)
        cross_p.append(trace_m * e_parts[i] - me + trace_n * g_parts[i] - ng)
    return (jnp.stack(cross_q, axis=-4), jnp.stack(cross_p, axis=-4))

def reference(models, direction, coupling, tv_weight):
    grads = forward_diffs(models)
    dirs = forward_diffs(direction)
    moms = moments(grads, dirs, coupling)
    cross_q, cross_p = couple(moms, grads, dirs)
    size = jnp.sqrt(lax.optimization_barrier(jnp.sum(grads * grads, 1)) + EPS_SQ)[:, None]
    alpha = coupling[:, None, None, None, None]
    beta = tv_weight[:, None, None, None, None]
    gradient = adjoint(beta * grads / size + alpha * cross_q)
    hessian_vector = adjoint(beta * dirs / size + alpha * cross_p)
    return (gradient, hessian_vector)
```

```python
import functools

import jax
import jax.numpy as jnp
from jax import lax
from jax.experimental import pallas as pl
from jax.experimental.pallas import tpu as pltpu
from jax.sharding import PartitionSpec as P

EPS_SQ = 0.25
MESH = pl.DeviceIdType.MESH
MODELS = 8
CHIPS = 4
NZ = 16
ROWS = 16
LANES = 128
SLABS = 38
COLS = 36

RING = ("O0", "O1", "B0", "B1", "HO", "HB", "F0", "F1", "FH")
NAMES = (
    ["ty0", "ty1", "tx0", "tx1", "S1", "S0", "SH"]
    + [d + k for d in "+-" for k in RING]
    + ["X" + d + k for d in "+-" for k in RING]
    + ["P%d%d" % (a, b) for a in range(CHIPS) for b in range(2) if a + b > 0]
)
INDEX = {name: i for i, name in enumerate(NAMES)}


def kernel(
    x_hbm, d_hbm, coupling, tv_weight, gout, hout,
    held, tile, moms, own_cols, got_cols, col_flux, in_sem, send_sem, recv_sem,
):
    mp, tx, ty = (lax.axis_index(a) for a in ("mp", "tx", "ty"))
    n_tx, n_ty = lax.axis_size("tx"), lax.axis_size("ty")
    chip, core = mp // 2, mp % 2
    sib = 1 - core

    def at_chip(by):
        return lax.rem(chip + by + CHIPS, CHIPS)

    def peer(by, other):
        return (at_chip(by) * 2 + (sib if other else core), tx, ty)

    left = (mp, lax.rem(tx + n_tx - 1, n_tx), ty)
    right = (mp, lax.rem(tx + 1, n_tx), ty)
    before = (mp, tx, lax.rem(ty + n_ty - 1, n_ty))
    after = (mp, tx, lax.rem(ty + 1, n_ty))
    peers = [(a, b) for a in range(CHIPS) for b in range(2) if a + b > 0]

    loads = [
        pltpu.make_async_copy(x_hbm, tile.at[0], in_sem.at[0]),
        pltpu.make_async_copy(d_hbm, tile.at[1], in_sem.at[1]),
    ]
    for load in loads:
        load.start()
    barrier = pltpu.get_barrier_semaphore()
    everyone = [peer(a, b) for a, b in peers] + [left, right, before, after]
    for device in everyone:
        pl.semaphore_signal(barrier, inc=1, device_id=device, device_id_type=MESH)

    lane = lax.broadcasted_iota(jnp.int32, (NZ, LANES), 1)
    level = lax.broadcasted_iota(jnp.int32, (NZ, LANES), 0)
    inner_z = level < NZ - 1

    started = []

    def copy(name, src, dst, device):
        i = INDEX[name]
        return pltpu.make_async_remote_copy(
            src_ref=src, dst_ref=dst, send_sem=send_sem.at[i], recv_sem=recv_sem.at[i],
            device_id=device, device_id_type=MESH,
        )

    def send(name, src, device, dst=None):
        c = copy(name, src, src if dst is None else dst, device)
        c.start()
        started.append(c)

    def arrived(name, dst):
        copy(name, dst, dst, peer(0, 1)).wait_recv()

    def piece(owner_chip, owner_core, half, kind):
        model = owner_chip * 2 + owner_core
        if kind == "h":
            return held.at[model, pl.ds(2 - 2 * half, 2)]
        if kind == "all":
            return held.at[model, pl.ds(4 + 16 * half, 16)]
        return held.at[model, pl.ds(4 + 16 * half + 8 * kind, 8)]

    def pack_row(cols, q, r):
        v = held[mp, 2 * ((r + 2) % 18) + q]
        low = pltpu.roll(v, (r + 2) % LANES, 1)
        high = pltpu.roll(v, (r + 97) % LANES, 1)
        cols = jnp.where(lane == r + 1, low, cols)
        return jnp.where(lane == r + 97, high, cols)

    for load in loads:
        load.wait()
    for q in range(2):
        cols = jnp.zeros((NZ, LANES), jnp.float32)
        for r in range(ROWS):
            held[mp, 2 * (r + 2) + q] = tile[q, pl.ds(r, NZ, stride=ROWS), :]
        for r in range(ROWS):
            cols = pack_row(cols, q, r)
        own_cols[q] = cols

    pl.semaphore_wait(barrier, len(everyone))

    send("ty0", held.at[mp, pl.ds(4, 2)], before, held.at[mp, pl.ds(0, 2)])
    send("ty1", held.at[mp, pl.ds(34, 2)], after, held.at[mp, pl.ds(2, 2)])
    send("S1", piece(chip, core, sib, "all"), peer(0, 1))
    send("+O0", piece(chip, core, core, 0), peer(1, 0))
    send("-O1", piece(chip, core, core, 1), peer(-1, 0))
    send("+O1", piece(chip, core, core, 1), peer(1, 0))
    send("-O0", piece(chip, core, core, 0), peer(-1, 0))
    send("S0", piece(chip, core, core, "all"), peer(0, 1))
    arrived("S1", piece(chip, sib, core, "all"))
    send("+B0", piece(chip, sib, core, 0), peer(1, 0))
    send("-B1", piece(chip, sib, core, 1), peer(-1, 0))
    send("+B1", piece(chip, sib, core, 1), peer(1, 0))
    send("-B0", piece(chip, sib, core, 0), peer(-1, 0))
    arrived("S0", piece(chip, sib, sib, "all"))

    def differences(f, f_next, keep_y=None):
        dx = pltpu.roll(f, LANES - 1, 1) - f
        dy = f_next - f
        if keep_y is not None:
            dy = dy * keep_y
        dz = jnp.where(inner_z, pltpu.roll(f, NZ - 1, 0) - f, 0.0)
        return dx, dy, dz

    def row_fields(model, i):
        here = 2 * (i + 1)
        then = 2 * jnp.where(i == ROWS, 0, i + 2)
        keep = jnp.where((i == ROWS) & (ty == n_ty - 1), 0.0, 1.0)
        g = differences(held[model, here], held[model, then], keep)
        e = differences(held[model, here + 1], held[model, then + 1], keep)
        return g, e

    def add_moments(acc, g, e, weight):
        w = [weight * v for v in g]
        terms = [w[0] * g[0], w[1] * g[1], w[2] * g[2], w[0] * g[1], w[0] * g[2], w[1] * g[2]]
        terms += [e[i] * w[j] for i in range(3) for j in range(3)]
        return terms if acc is None else [a + t for a, t in zip(acc, terms)]

    def gather_rows(models, first, last, fresh):
        def body(i, carry):
            acc = None if fresh else [moms[i, j] for j in range(15)]
            for model in models:
                g, e = row_fields(model, i)
                acc = add_moments(acc, g, e, coupling[model])
            for j in range(15):
                moms[i, j] = acc[j]
            return carry

        lax.fori_loop(first, last, body, 0)

    pair_own = [chip * 2, chip * 2 + 1]
    pair_prev = [at_chip(-1) * 2, at_chip(-1) * 2 + 1]
    pair_next = [at_chip(1) * 2, at_chip(1) * 2 + 1]
    pair_far = [at_chip(2) * 2, at_chip(2) * 2 + 1]

    gather_rows(pair_own, 1, ROWS, True)

    arrived("ty0", held.at[mp, pl.ds(0, 2)])
    arrived("ty1", held.at[mp, pl.ds(2, 2)])
    send("SH", held.at[mp, pl.ds(0, 4)], peer(0, 1))
    send("+HO", piece(chip, core, core, "h"), peer(1, 0))
    send("-HO", piece(chip, core, core, "h"), peer(-1, 0))
    for q in range(2):
        own_cols[q] = pack_row(pack_row(own_cols[q], q, -1), q, ROWS)
    send("tx0", own_cols, left, got_cols.at[0])
    send("tx1", own_cols, right, got_cols.at[1])

    def relay(d, kind, source, owner_core, half_piece):
        ref = piece(source, owner_core, core, half_piece)
        arrived(d + kind, ref)
        send("X" + d + kind, ref, peer(0, 1))
        return ref

    prev, nxt, far = at_chip(-1), at_chip(1), at_chip(2)
    send("+F0", relay("+", "O0", prev, core, 0), peer(1, 0))
    send("-F0", relay("-", "O1", nxt, core, 1), peer(-1, 0))
    arrived("SH", held.at[chip * 2 + sib, pl.ds(0, 4)])
    send("+HB", piece(chip, sib, core, "h"), peer(1, 0))
    send("-HB", piece(chip, sib, core, "h"), peer(-1, 0))
    relay("+", "O1", prev, core, 1)
    relay("-", "O0", nxt, core, 0)
    send("+F1", relay("+", "B0", prev, sib, 0), peer(1, 0))
    send("-F1", relay("-", "B1", nxt, sib, 1), peer(-1, 0))
    relay("+", "B1", prev, sib, 1)
    relay("-", "B0", nxt, sib, 0)
    send("+FH", relay("+", "HO", prev, core, "h"), peer(1, 0))
    relay("-", "HO", nxt, core, "h")
    relay("+", "HB", prev, sib, "h")
    send("-FH", relay("-", "HB", nxt, sib, "h"), peer(-1, 0))

    arrived("tx0", got_cols.at[0])
    arrived("tx1", got_cols.at[1])
    for q in range(2):
        mine = own_cols[q]
        cols = jnp.where(lane < 64, pltpu.roll(got_cols[1, q], 32, 1), pltpu.roll(got_cols[0, q], 96, 1))
        held[mp, COLS + q] = jnp.where((lane < 32) | (lane >= 96), mine, cols)
    for a, b in peers:
        send("P%d%d" % (a, b), held.at[mp, pl.ds(COLS, 2)], peer(a, b))

    for d, source in (("+", prev), ("-", nxt)):
        for kind, other, half_piece in (
            ("O0", 1, 0), ("O1", 1, 1), ("B0", 0, 0), ("B1", 0, 1), ("HO", 1, "h"), ("HB", 0, "h"),
        ):
            owner = sib if other else core
            arrived("X" + d + kind, piece(source, owner, sib, half_piece))

    gather_rows(pair_own, ROWS, ROWS + 1, True)
    gather_rows(pair_own, 0, 1, True)
    gather_rows(pair_prev + pair_next, 0, ROWS + 1, False)

    relay("+", "F0", far, core, 0)
    relay("-", "F0", far, core, 1)
    relay("+", "F1", far, sib, 0)
    relay("-", "F1", far, sib, 1)
    relay("+", "FH", far, core, "h")
    relay("-", "FH", far, sib, "h")
    arrived("X+F0", piece(far, sib, sib, 0))
    arrived("X-F0", piece(far, sib, sib, 1))
    arrived("X+F1", piece(far, core, sib, 0))
    arrived("X-F1", piece(far, core, sib, 1))
    arrived("X+FH", piece(far, sib, sib, "h"))
    arrived("X-FH", piece(far, core, sib, "h"))

    for a, b in peers:
        owner = at_chip(-a) * 2 + (sib if b else core)
        arrived("P%d%d" % (a, b), held.at[owner, pl.ds(COLS, 2)])

    alpha = coupling[mp]
    ratio = tv_weight[mp] / alpha

    def fluxes(m, g, e):
        size_sq = g[0] * g[0] + g[1] * g[1] + g[2] * g[2] + EPS_SQ
        tv = ratio * lax.rsqrt(size_sq)
        a00, a11, a22 = m[1] + m[2] + tv, m[0] + m[2] + tv, m[0] + m[1] + tv
        b00, b11, b22 = m[10] + m[14], m[6] + m[14], m[6] + m[10]
        q = (
            a00 * g[0] - (m[3] * g[1] + m[4] * g[2]),
            a11 * g[1] - (m[3] * g[0] + m[5] * g[2]),
            a22 * g[2] - (m[4] * g[0] + m[5] * g[1]),
        )
        p = (
            (a00 * e[0] + b00 * g[0]) - ((m[3] * e[1] + m[4] * e[2]) + (m[7] * g[1] + m[8] * g[2])),
            (a11 * e[1] + b11 * g[1]) - ((m[3] * e[0] + m[5] * e[2]) + (m[9] * g[0] + m[11] * g[2])),
            (a22 * e[2] + b22 * g[2]) - ((m[4] * e[0] + m[5] * e[1]) + (m[12] * g[0] + m[13] * g[1])),
        )
        return q, p

    def along_z(fz):
        fz = jnp.where(inner_z, fz, 0.0)
        return jnp.where(level == 0, 0.0, pltpu.roll(fz, 1, 0)) - fz

    no_x = (lane < 32) & (tx == n_tx - 1)
    no_y = ((lane == ROWS) | (lane == ROWS + 32)) & (ty == n_ty - 1)

    def col_fields(model):
        out = []
        for q in range(2):
            v = held[model, COLS + q]
            dx = jnp.where(no_x, 0.0, pltpu.roll(v, 64, 1) - v)
            dy = jnp.where(no_y, 0.0, pltpu.roll(v, LANES - 1, 1) - v)
            dz = jnp.where(inner_z, pltpu.roll(v, NZ - 1, 0) - v, 0.0)
            out.append((dx, dy, dz))
        return out

    def col_body(model, acc):
        g, e = col_fields(model)
        return tuple(add_moments(acc, g, e, coupling[model]))

    zero = jnp.zeros((NZ, LANES), jnp.float32)
    col_moms = lax.fori_loop(0, MODELS, col_body, (zero,) * 15)
    off_x = no_x | ((lane >= 32) & (tx == 0))
    off_y = no_y | ((lane == 0) & (ty == 0))
    ends, starts = [], []
    for f in fluxes(col_moms, *col_fields(mp)):
        fx = jnp.where(off_x, 0.0, f[0])
        fy = jnp.where(off_y, 0.0, f[1])
        ends.append(pltpu.roll(fy, 1, 1) - fy + along_z(f[2]) - fx)
        starts.append(fx)
    for q in range(2):
        col_flux[0, q] = ends[q]
        col_flux[1, q] = starts[q]

    outs = (gout, hout)

    def row_flux(i):
        acc = [moms[i, j] for j in range(15)]
        for model in pair_far:
            g, e = row_fields(model, i)
            acc = add_moments(acc, g, e, coupling[model])
        return fluxes(acc, *row_fields(mp, i))

    first = row_flux(0)
    keep_first = jnp.where(ty == 0, 0.0, 1.0)
    carry = tuple(f[1] * keep_first for f in first)

    def out_body(r, carry):
        both = row_flux(r + 1)
        keep = jnp.where((r == ROWS - 1) & (ty == n_ty - 1), 0.0, 1.0)
        new = []
        for q in range(2):
            fx, fy, fz = both[q]
            fy = fy * keep
            before_x = jnp.where(lane == 0, pltpu.roll(col_flux[1, q], 95 - r, 1), pltpu.roll(fx, 1, 1))
            rest = carry[q] - fy + along_z(fz) - fx
            rest = jnp.where(lane == LANES - 1, pltpu.roll(col_flux[0, q], 126 - r, 1), rest)
            outs[q][pl.ds(r, NZ, stride=ROWS), :] = alpha * (before_x + rest)
            new.append(fy)
        return tuple(new)

    lax.fori_loop(0, ROWS, out_body, carry)

    for c in started:
        c.wait_send()


def shards(models, direction, coupling, tv_weight):
    flat = (NZ * ROWS, LANES)
    n = len(NAMES)
    out = pl.pallas_call(
        kernel,
        name="fused",
        out_shape=[jax.ShapeDtypeStruct(flat, jnp.float32)] * 2,
        in_specs=[pl.BlockSpec(memory_space=pl.ANY)] * 2 + [pl.BlockSpec(memory_space=pltpu.SMEM)] * 2,
        out_specs=[pl.BlockSpec(memory_space=pltpu.VMEM)] * 2,
        scratch_shapes=[
            pltpu.VMEM((MODELS, SLABS, NZ, LANES), jnp.float32),
            pltpu.VMEM((2,) + flat, jnp.float32),
            pltpu.VMEM((ROWS + 1, 15, NZ, LANES), jnp.float32),
            pltpu.VMEM((2, NZ, LANES), jnp.float32),
            pltpu.VMEM((2, 2, NZ, LANES), jnp.float32),
            pltpu.VMEM((2, 2, NZ, LANES), jnp.float32),
            pltpu.SemaphoreType.DMA((2,)),
            pltpu.SemaphoreType.DMA((n,)),
            pltpu.SemaphoreType.DMA((n,)),
        ],
        compiler_params=pltpu.CompilerParams(
            collective_id=1, has_side_effects=True, vmem_limit_bytes=60 * 2**20
        ),
    )(models.reshape(flat), direction.reshape(flat), coupling, tv_weight)
    return tuple(o.reshape(models.shape) for o in out)


def solution(mesh):
    placed = (P("mp", None, "ty", "tx"), P("mp", None, "ty", "tx"), P(), P())
    return jax.shard_map(
        shards,
        mesh=mesh,
        in_specs=placed,
        out_specs=(P("mp", None, "ty", "tx"), P("mp", None, "ty", "tx")),
        check_vma=False,
    )
```

```python
import functools

import jax
import jax.numpy as jnp
from jax import lax
from jax.experimental import pallas as pl
from jax.experimental.pallas import tpu as pltpu
from jax.sharding import PartitionSpec as P

EPS_SQ = 0.25
MESH = pl.DeviceIdType.MESH
MODELS = 8
CHIPS = 4
NZ = 16
ROWS = 16
LANES = 128
SLABS = 38
COLS = 36

RING = ("O0", "O1", "B0", "B1", "HO", "HB", "F0", "F1", "FH")
NAMES = (
    ["ty0", "ty1", "tx0", "tx1", "S1", "S0", "SH"]
    + [d + k for d in "+-" for k in RING]
    + ["X" + d + k for d in "+-" for k in RING]
    + ["P%d%d" % (a, b) for a in range(CHIPS) for b in range(2) if a + b > 0]
)
INDEX = {name: i for i, name in enumerate(NAMES)}


def kernel(
    x_hbm, d_hbm, coupling_hbm, tv_hbm, gout, hout,
    held, tile, moms, own_cols, got_cols, col_flux, coupling, tv_weight, in_sem, send_sem, recv_sem, leave,
):
    mp, tx, ty = (lax.axis_index(a) for a in ("mp", "tx", "ty"))
    n_tx, n_ty = lax.axis_size("tx"), lax.axis_size("ty")
    chip, core = mp // 2, mp % 2
    sib = 1 - core

    def at_chip(by):
        return lax.rem(chip + by + CHIPS, CHIPS)

    def peer(by, other):
        return (at_chip(by) * 2 + (sib if other else core), tx, ty)

    left, right = (mp, jnp.maximum(tx - 1, 0), ty), (mp, jnp.minimum(tx + 1, n_tx - 1), ty)
    before, after = (mp, tx, jnp.maximum(ty - 1, 0)), (mp, tx, jnp.minimum(ty + 1, n_ty - 1))
    has_left, has_right, has_before, has_after = tx > 0, tx < n_tx - 1, ty > 0, ty < n_ty - 1
    greets_left, greeted_right = tx == n_tx - 1, tx == n_tx - 2
    gives_leave = has_left & jnp.logical_not(greets_left)
    needs_leave = has_right & jnp.logical_not(greeted_right)
    peers = [(a, b) for a in range(CHIPS) for b in range(2) if a + b > 0]

    barrier = pltpu.get_barrier_semaphore()

    def greet(device):
        pl.semaphore_signal(barrier, inc=1, device_id=device, device_id_type=MESH)

    for wanted, device in ((has_before, before), (has_after, after), (has_right, right), (greets_left, left)):
        pl.when(wanted)(functools.partial(greet, device))
    for a, b in peers:
        greet(peer(a, b))
    loads = [
        pltpu.make_async_copy(src, dst, in_sem.at[i])
        for i, (src, dst) in enumerate(
            ((x_hbm, tile.at[0]), (d_hbm, tile.at[1]), (coupling_hbm, coupling), (tv_hbm, tv_weight))
        )
    ]
    for load in loads:
        load.start()

    lane = lax.broadcasted_iota(jnp.int32, (NZ, LANES), 1)
    level = lax.broadcasted_iota(jnp.int32, (NZ, LANES), 0)
    inner_z = level < NZ - 1
    zero = jnp.zeros((NZ, LANES), jnp.float32)

    started = []

    def copy(name, src, dst, device):
        i = INDEX[name]
        return pltpu.make_async_remote_copy(
            src_ref=src, dst_ref=dst, send_sem=send_sem.at[i], recv_sem=recv_sem.at[i],
            device_id=device, device_id_type=MESH,
        )

    def send(name, src, device, dst=None, wanted=None):
        c = copy(name, src, src if dst is None else dst, device)
        if wanted is None:
            c.start()
        else:
            pl.when(wanted)(c.start)
        started.append((wanted, c))

    def arrived(name, dst, wanted=None):
        wait = copy(name, dst, dst, peer(0, 1)).wait_recv
        if wanted is None:
            wait()
        else:
            pl.when(wanted)(wait)

    def piece(owner_chip, owner_core, half, kind):
        model = owner_chip * 2 + owner_core
        if kind == "h":
            return held.at[model, pl.ds(2 - 2 * half, 2)]
        if kind == "all":
            return held.at[model, pl.ds(4 + 16 * half, 16)]
        return held.at[model, pl.ds(4 + 16 * half + 8 * kind, 8)]

    def pack_row(cols, q, r):
        v = held[mp, 2 * ((r + 2) % 18) + q]
        low = pltpu.roll(v, (r + 2) % LANES, 1)
        high = pltpu.roll(v, (r + 97) % LANES, 1)
        cols = jnp.where(lane == r + 1, low, cols)
        return jnp.where(lane == r + 97, high, cols)

    def blank(ref):
        ref[...] = jnp.zeros(ref.shape, jnp.float32)

    rim_after, rim_before = held.at[mp, pl.ds(0, 2)], held.at[mp, pl.ds(2, 2)]
    for missing, ref in (
        (jnp.logical_not(has_after), rim_after), (jnp.logical_not(has_before), rim_before),
        (jnp.logical_not(has_right), got_cols.at[0]), (jnp.logical_not(has_left), got_cols.at[1]),
    ):
        pl.when(missing)(functools.partial(blank, ref))
    for load in loads:
        load.wait()
    for q in range(2):
        for r in range(ROWS):
            held[mp, 2 * (r + 2) + q] = tile[q, pl.ds(r, NZ, stride=ROWS), :]
    for q in range(2):
        cols = zero
        for r in range(ROWS):
            cols = pack_row(cols, q, r)
        own_cols[q] = cols

    expected = len(peers) + sum(w.astype(jnp.int32) for w in (has_before, has_after, has_left, greeted_right))
    pl.semaphore_wait(barrier, expected)

    send("ty0", held.at[mp, pl.ds(4, 2)], before, rim_after, has_before)
    send("ty1", held.at[mp, pl.ds(34, 2)], after, rim_before, has_after)
    send("S1", piece(chip, core, sib, "all"), peer(0, 1))
    send("+O0", piece(chip, core, core, 0), peer(1, 0))
    send("-O1", piece(chip, core, core, 1), peer(-1, 0))
    send("+O1", piece(chip, core, core, 1), peer(1, 0))
    send("-O0", piece(chip, core, core, 0), peer(-1, 0))
    send("S0", piece(chip, core, core, "all"), peer(0, 1))

    def give_leave():
        pl.semaphore_signal(leave, inc=1, device_id=left, device_id_type=MESH)

    pl.when(gives_leave)(give_leave)
    arrived("S1", piece(chip, sib, core, "all"))
    send("+B0", piece(chip, sib, core, 0), peer(1, 0))
    send("-B1", piece(chip, sib, core, 1), peer(-1, 0))
    send("+B1", piece(chip, sib, core, 1), peer(1, 0))
    send("-B0", piece(chip, sib, core, 0), peer(-1, 0))
    arrived("S0", piece(chip, sib, sib, "all"))

    def differences(f, f_next, keep_y=None):
        dx = pltpu.roll(f, LANES - 1, 1) - f
        dy = f_next - f
        if keep_y is not None:
            dy = dy * keep_y
        dz = jnp.where(inner_z, pltpu.roll(f, NZ - 1, 0) - f, 0.0)
        return dx, dy, dz

    keep_last = jnp.where(has_after, 1.0, 0.0)

    def row_fields(model, i):
        here = 2 * (i + 1)
        last = isinstance(i, int) and i == ROWS
        then = 0 if last else 2 * (i + 2)
        keep = keep_last if last else None
        g = differences(held[model, here], held[model, then], keep)
        e = differences(held[model, here + 1], held[model, then + 1], keep)
        return g, e

    def add_moments(acc, g, e, weight):
        w = [weight * v for v in g]
        terms = [w[0] * g[0], w[1] * g[1], w[2] * g[2], w[0] * g[1], w[0] * g[2], w[1] * g[2]]
        terms += [e[i] * w[j] for i in range(3) for j in range(3)]
        return terms if acc is None else [a + t for a, t in zip(acc, terms)]

    def row_moments(acc, models, i):
        for model in models:
            g, e = row_fields(model, i)
            acc = add_moments(acc, g, e, coupling[model])
        return acc

    def gather_rows(models, fresh):
        def body(i, carry):
            acc = row_moments(None if fresh else [moms[i, j] for j in range(15)], models, i)
            for j in range(15):
                moms[i, j] = acc[j]
            return carry

        lax.fori_loop(1, ROWS, body, 0, unroll=5)

    prev, nxt, far = at_chip(-1), at_chip(1), at_chip(2)
    pair_own, pair_prev, pair_next, pair_far = ([c * 2, c * 2 + 1] for c in (chip, prev, nxt, far))

    def relay(d, kind, source, owner_core, half_piece):
        ref = piece(source, owner_core, core, half_piece)
        arrived(d + kind, ref)
        send("X" + d + kind, ref, peer(0, 1))
        return ref

    gather_rows(pair_own, True)

    send("+F0", relay("+", "O0", prev, core, 0), peer(1, 0))
    send("-F0", relay("-", "O1", nxt, core, 1), peer(-1, 0))
    arrived("ty0", rim_after, has_after)
    arrived("ty1", rim_before, has_before)
    send("SH", held.at[mp, pl.ds(0, 4)], peer(0, 1))
    send("+HO", piece(chip, core, core, "h"), peer(1, 0))
    send("-HO", piece(chip, core, core, "h"), peer(-1, 0))
    for q in range(2):
        own_cols[q] = pack_row(pack_row(own_cols[q], q, -1), q, ROWS)
    send("tx0", own_cols, left, got_cols.at[0], has_left)
    to_right = copy("tx1", own_cols, got_cols.at[1], right)
    pl.when(greeted_right)(to_right.start)
    started.append((has_right, to_right))
    relay("+", "O1", prev, core, 1)
    relay("-", "O0", nxt, core, 0)
    arrived("SH", held.at[chip * 2 + sib, pl.ds(0, 4)])
    send("+HB", piece(chip, sib, core, "h"), peer(1, 0))
    send("-HB", piece(chip, sib, core, "h"), peer(-1, 0))
    send("+F1", relay("+", "B0", prev, sib, 0), peer(1, 0))
    send("-F1", relay("-", "B1", nxt, sib, 1), peer(-1, 0))
    relay("+", "B1", prev, sib, 1)
    relay("-", "B0", nxt, sib, 0)
    send("+FH", relay("+", "HO", prev, core, "h"), peer(1, 0))
    relay("-", "HO", nxt, core, "h")
    relay("+", "HB", prev, sib, "h")
    send("-FH", relay("-", "HB", nxt, sib, "h"), peer(-1, 0))

    for d, source in (("+", prev), ("-", nxt)):
        for kind, owner, half_piece in (("O0", sib, 0), ("O1", sib, 1), ("B0", core, 0), ("B1", core, 1)):
            arrived("X" + d + kind, piece(source, owner, sib, half_piece))
    gather_rows(pair_prev + pair_next, False)

    def go_right():
        pl.semaphore_wait(leave, 1)
        to_right.start()

    pl.when(needs_leave)(go_right)

    relay("+", "F0", far, core, 0)
    relay("-", "F0", far, core, 1)
    relay("+", "F1", far, sib, 0)
    relay("-", "F1", far, sib, 1)
    relay("+", "FH", far, core, "h")
    relay("-", "FH", far, sib, "h")

    arrived("tx0", got_cols.at[0], has_right)
    arrived("tx1", got_cols.at[1], has_left)
    for q in range(2):
        mine = own_cols[q]
        cols = jnp.where(lane < 64, pltpu.roll(got_cols[1, q], 32, 1), pltpu.roll(got_cols[0, q], 96, 1))
        held[mp, COLS + q] = jnp.where((lane < 32) | (lane >= 96), mine, cols)
    for a, b in peers:
        send("P%d%d" % (a, b), held.at[mp, pl.ds(COLS, 2)], peer(a, b))

    alpha = coupling[mp]
    ratio = tv_weight[mp] / alpha

    def fluxes(m, g, e):
        size_sq = g[0] * g[0] + g[1] * g[1] + g[2] * g[2] + EPS_SQ
        tv = ratio * lax.rsqrt(size_sq)
        a00, a11, a22 = m[1] + m[2] + tv, m[0] + m[2] + tv, m[0] + m[1] + tv
        b00, b11, b22 = m[10] + m[14], m[6] + m[14], m[6] + m[10]
        q = (
            a00 * g[0] - (m[3] * g[1] + m[4] * g[2]),
            a11 * g[1] - (m[3] * g[0] + m[5] * g[2]),
            a22 * g[2] - (m[4] * g[0] + m[5] * g[1]),
        )
        p = (
            (a00 * e[0] + b00 * g[0]) - ((m[3] * e[1] + m[4] * e[2]) + (m[7] * g[1] + m[8] * g[2])),
            (a11 * e[1] + b11 * g[1]) - ((m[3] * e[0] + m[5] * e[2]) + (m[9] * g[0] + m[11] * g[2])),
            (a22 * e[2] + b22 * g[2]) - ((m[4] * e[0] + m[5] * e[1]) + (m[12] * g[0] + m[13] * g[1])),
        )
        return q, p

    def along_z(fz):
        fz = jnp.where(inner_z, fz, 0.0)
        return jnp.where(level == 0, 0.0, pltpu.roll(fz, 1, 0)) - fz

    outs = (gout, hout)

    def put_row(i, both, before_y, keep=None):
        new = []
        for q in range(2):
            fx, fy, fz = both[q]
            if keep is not None:
                fy = fy * keep
            enters = jnp.where(lane == 0, 0.0, pltpu.roll(fx, 1, 1))
            rest = jnp.where(lane == LANES - 1, 0.0, before_y[q] - fy + along_z(fz) - fx)
            outs[q][pl.ds(i - 1, NZ, stride=ROWS), :] = alpha * (enters + rest)
            new.append(fy)
        return tuple(new)

    for name, owner, half_piece in (
        ("X+F0", sib, 0), ("X-F0", sib, 1), ("X+F1", core, 0), ("X-F1", core, 1),
    ):
        arrived(name, piece(far, owner, sib, half_piece))

    def out_body(i, carry):
        acc = row_moments([moms[i, j] for j in range(15)], pair_far, i)
        return put_row(i, fluxes(acc, *row_fields(mp, i)), carry)

    carry = lax.fori_loop(1, ROWS, out_body, (zero, zero), unroll=5)

    for d, source in (("+", prev), ("-", nxt)):
        arrived("X" + d + "HO", piece(source, sib, sib, "h"))
        arrived("X" + d + "HB", piece(source, core, sib, "h"))
    arrived("X+FH", piece(far, sib, sib, "h"))
    arrived("X-FH", piece(far, core, sib, "h"))
    every = pair_own + pair_prev + pair_next + pair_far
    put_row(ROWS, fluxes(row_moments(None, every, ROWS), *row_fields(mp, ROWS)), carry, keep_last)
    keep_first = alpha * jnp.where(has_before, 1.0, 0.0)
    entering = [f[1] * keep_first for f in fluxes(row_moments(None, every, 0), *row_fields(mp, 0))]

    for a, b in peers:
        owner = at_chip(-a) * 2 + (sib if b else core)
        arrived("P%d%d" % (a, b), held.at[owner, pl.ds(COLS, 2)])
    no_x = (lane < 32) & (tx == n_tx - 1)
    no_y = ((lane == ROWS) | (lane == ROWS + 32)) & (ty == n_ty - 1)

    def col_fields(model):
        out = []
        for q in range(2):
            v = held[model, COLS + q]
            dx = jnp.where(no_x, 0.0, pltpu.roll(v, 64, 1) - v)
            dy = jnp.where(no_y, 0.0, pltpu.roll(v, LANES - 1, 1) - v)
            dz = jnp.where(inner_z, pltpu.roll(v, NZ - 1, 0) - v, 0.0)
            out.append((dx, dy, dz))
        return out

    col_moms = None
    for model in range(MODELS):
        g, e = col_fields(model)
        col_moms = add_moments(col_moms, g, e, coupling[model])
    off_x = no_x | ((lane >= 32) & (tx == 0))
    off_y = no_y | ((lane == 0) & (ty == 0))
    for q, f in enumerate(fluxes(col_moms, *col_fields(mp))):
        fx = jnp.where(off_x, 0.0, f[0])
        fy = jnp.where(off_y, 0.0, f[1])
        col_flux[0, q] = alpha * (pltpu.roll(fy, 1, 1) - fy + along_z(f[2]) - fx)
        col_flux[1, q] = alpha * fx
    for q in range(2):
        ends, starts = col_flux[0, q], col_flux[1, q]
        for r in range(ROWS):
            rows = pl.ds(r, NZ, stride=ROWS)
            more = jnp.where(lane == LANES - 1, pltpu.roll(ends, 126 - r, 1), 0.0)
            more = jnp.where(lane == 0, pltpu.roll(starts, 95 - r, 1), more)
            if r == 0:
                more = more + jnp.where(lane == LANES - 1, 0.0, entering[q])
            outs[q][rows, :] = outs[q][rows, :] + more

    for wanted, c in started:
        if wanted is None:
            c.wait_send()
        else:
            pl.when(wanted)(c.wait_send)


def shards(models, direction, coupling, tv_weight):
    flat = (NZ * ROWS, LANES)
    n = len(NAMES)
    out = pl.pallas_call(
        kernel,
        name="fused",
        out_shape=[jax.ShapeDtypeStruct(flat, jnp.float32)] * 2,
        in_specs=[pl.BlockSpec(memory_space=pl.ANY)] * 4,
        out_specs=[pl.BlockSpec(memory_space=pltpu.VMEM)] * 2,
        scratch_shapes=[
            pltpu.VMEM((MODELS, SLABS, NZ, LANES), jnp.float32),
            pltpu.VMEM((2,) + flat, jnp.float32),
            pltpu.VMEM((ROWS + 1, 15, NZ, LANES), jnp.float32),
            pltpu.VMEM((2, NZ, LANES), jnp.float32),
            pltpu.VMEM((2, 2, NZ, LANES), jnp.float32),
            pltpu.VMEM((2, 2, NZ, LANES), jnp.float32),
            pltpu.SMEM((MODELS,), jnp.float32),
            pltpu.SMEM((MODELS,), jnp.float32),
            pltpu.SemaphoreType.DMA((4,)),
            pltpu.SemaphoreType.DMA((n,)),
            pltpu.SemaphoreType.DMA((n,)),
            pltpu.SemaphoreType.REGULAR,
        ],
        compiler_params=pltpu.CompilerParams(
            collective_id=1, has_side_effects=True, vmem_limit_bytes=60 * 2**20
        ),
    )(models.reshape(flat), direction.reshape(flat), coupling, tv_weight)
    return tuple(o.reshape(models.shape) for o in out)


def solution(mesh):
    placed = (P("mp", None, "ty", "tx"), P("mp", None, "ty", "tx"), P(), P())
    return jax.shard_map(
        shards,
        mesh=mesh,
        in_specs=placed,
        out_specs=(P("mp", None, "ty", "tx"), P("mp", None, "ty", "tx")),
        check_vma=False,
    )
```

```python
import functools

import jax
import jax.numpy as jnp
from jax import lax
from jax.experimental import pallas as pl
from jax.experimental.pallas import tpu as pltpu
from jax.sharding import PartitionSpec as P

EPS_SQ = 0.25
MESH = pl.DeviceIdType.MESH
MODELS = 8
CHIPS = 4
NZ = 16
ROWS = 16
LANES = 128
SLABS = 38
COLS = 36

RING = ("O0", "O1", "O2", "O3", "H", "F0", "F1")
NAMES = (
    ["ty0", "ty1", "tx0", "tx1", "S", "SH"]
    + [d + k for d in "+-" for k in RING] + ["2H"]
    + ["X" + d + k for d in "+-" for k in RING] + ["X2H"]
    + ["P%d%d" % (a, b) for a in range(CHIPS) for b in range(2) if a + b > 0]
)
INDEX = {name: i for i, name in enumerate(NAMES)}


def kernel(
    x_hbm, d_hbm, coupling_hbm, tv_hbm, gout, hout,
    held, tile, moms, own_cols, got_cols, col_flux, coupling, tv_weight, in_sem, send_sem, recv_sem, leave,
):
    mp, tx, ty = (lax.axis_index(a) for a in ("mp", "tx", "ty"))
    n_tx, n_ty = lax.axis_size("tx"), lax.axis_size("ty")
    chip, core = mp // 2, mp % 2
    sib = 1 - core

    def at_chip(by):
        return lax.rem(chip + by + CHIPS, CHIPS)

    def peer(by, other):
        return (at_chip(by) * 2 + (sib if other else core), tx, ty)

    left, right = (mp, jnp.maximum(tx - 1, 0), ty), (mp, jnp.minimum(tx + 1, n_tx - 1), ty)
    before, after = (mp, tx, jnp.maximum(ty - 1, 0)), (mp, tx, jnp.minimum(ty + 1, n_ty - 1))
    has_left, has_right, has_before, has_after = tx > 0, tx < n_tx - 1, ty > 0, ty < n_ty - 1
    greets_left, greeted_right = tx == n_tx - 1, tx == n_tx - 2
    gives_leave = has_left & jnp.logical_not(greets_left)
    needs_leave = has_right & jnp.logical_not(greeted_right)
    peers = [(a, b) for a in range(CHIPS) for b in range(2) if a + b > 0]

    barrier = pltpu.get_barrier_semaphore()

    def greet(device):
        pl.semaphore_signal(barrier, inc=1, device_id=device, device_id_type=MESH)

    for wanted, device in ((has_before, before), (has_after, after), (has_right, right), (greets_left, left)):
        pl.when(wanted)(functools.partial(greet, device))
    for a, b in peers:
        greet(peer(a, b))
    loads = [
        pltpu.make_async_copy(src, dst, in_sem.at[i])
        for i, (src, dst) in enumerate(
            ((x_hbm, tile.at[0]), (d_hbm, tile.at[1]), (coupling_hbm, coupling), (tv_hbm, tv_weight))
        )
    ]
    for load in loads:
        load.start()

    lane = lax.broadcasted_iota(jnp.int32, (NZ, LANES), 1)
    level = lax.broadcasted_iota(jnp.int32, (NZ, LANES), 0)
    inner_z = level < NZ - 1
    zero = jnp.zeros((NZ, LANES), jnp.float32)

    started = []

    def copy(name, src, dst, device):
        i = INDEX[name]
        return pltpu.make_async_remote_copy(
            src_ref=src, dst_ref=dst, send_sem=send_sem.at[i], recv_sem=recv_sem.at[i],
            device_id=device, device_id_type=MESH,
        )

    def send(name, src, device, dst=None, wanted=None):
        c = copy(name, src, src if dst is None else dst, device)
        if wanted is None:
            c.start()
        else:
            pl.when(wanted)(c.start)
        started.append((wanted, c))

    def arrived(name, dst, wanted=None):
        wait = copy(name, dst, dst, peer(0, 1)).wait_recv
        if wanted is None:
            wait()
        else:
            pl.when(wanted)(wait)

    def piece(model, part):
        first, n = {"H": (0, 4), "all": (4, 32)}.get(part) or (4 + 8 * part, 8)
        return held.at[model, pl.ds(first, n)]

    def pack_row(cols, q, r):
        v = held[mp, 2 * ((r + 2) % 18) + q]
        low = pltpu.roll(v, (r + 2) % LANES, 1)
        high = pltpu.roll(v, (r + 97) % LANES, 1)
        cols = jnp.where(lane == r + 1, low, cols)
        return jnp.where(lane == r + 97, high, cols)

    def blank(ref):
        ref[...] = jnp.zeros(ref.shape, jnp.float32)

    rim_after, rim_before = held.at[mp, pl.ds(0, 2)], held.at[mp, pl.ds(2, 2)]
    for missing, ref in (
        (jnp.logical_not(has_after), rim_after), (jnp.logical_not(has_before), rim_before),
        (jnp.logical_not(has_right), got_cols.at[0]), (jnp.logical_not(has_left), got_cols.at[1]),
    ):
        pl.when(missing)(functools.partial(blank, ref))
    for load in loads:
        load.wait()
    for q in range(2):
        for r in range(ROWS):
            held[mp, 2 * (r + 2) + q] = tile[q, pl.ds(r, NZ, stride=ROWS), :]
    for q in range(2):
        cols = zero
        for r in range(ROWS):
            cols = pack_row(cols, q, r)
        own_cols[q] = cols

    expected = len(peers) + sum(w.astype(jnp.int32) for w in (has_before, has_after, has_left, greeted_right))
    pl.semaphore_wait(barrier, expected)

    send("ty0", held.at[mp, pl.ds(4, 2)], before, rim_after, has_before)
    send("ty1", held.at[mp, pl.ds(34, 2)], after, rim_before, has_after)
    for up, down in ((0, 2), (1, 3), (2, 0), (3, 1)):
        send("+O%d" % up, piece(mp, up), peer(1, 0))
        send("-O%d" % down, piece(mp, down), peer(-1, 0))
        if up == 1:
            send("S", piece(mp, "all"), peer(0, 1))

    def give_leave():
        pl.semaphore_signal(leave, inc=1, device_id=left, device_id_type=MESH)

    pl.when(gives_leave)(give_leave)
    arrived("S", piece(chip * 2 + sib, "all"))

    def differences(f, f_next, keep_y=None):
        dx = pltpu.roll(f, LANES - 1, 1) - f
        dy = f_next - f
        if keep_y is not None:
            dy = dy * keep_y
        dz = jnp.where(inner_z, pltpu.roll(f, NZ - 1, 0) - f, 0.0)
        return dx, dy, dz

    keep_last = jnp.where(has_after, 1.0, 0.0)

    def row_fields(model, i):
        here = 2 * (i + 1)
        last = isinstance(i, int) and i == ROWS
        then = 0 if last else 2 * (i + 2)
        keep = keep_last if last else None
        g = differences(held[model, here], held[model, then], keep)
        e = differences(held[model, here + 1], held[model, then + 1], keep)
        return g, e

    def add_moments(acc, g, e, weight):
        w = [weight * v for v in g]
        terms = [w[0] * g[0], w[1] * g[1], w[2] * g[2], w[0] * g[1], w[0] * g[2], w[1] * g[2]]
        terms += [e[i] * w[j] for i in range(3) for j in range(3)]
        return terms if acc is None else [a + t for a, t in zip(acc, terms)]

    def row_moments(acc, models, i):
        for model in models:
            g, e = row_fields(model, i)
            acc = add_moments(acc, g, e, coupling[model])
        return acc

    def gather_rows(models, fresh):
        def body(i, carry):
            acc = row_moments(None if fresh else [moms[i, j] for j in range(15)], models, i)
            for j in range(15):
                moms[i, j] = acc[j]
            return carry

        lax.fori_loop(1, ROWS, body, 0, unroll=5)

    prev, nxt, far = at_chip(-1), at_chip(1), at_chip(2)
    pair_own, pair_far = [chip * 2, chip * 2 + 1], [far * 2, far * 2 + 1]

    def relay(d, kind, source, part):
        ref = piece(source * 2 + core, part)
        arrived(d + kind, ref)
        send("X" + d + kind, ref, peer(0, 1))

    def onward(d, kind, source, part):
        send(d + kind, piece(source * 2 + core, part), peer(1 if d == "+" else -1, 0))

    def from_sibling(d, kind, source, part):
        arrived("X" + d + kind, piece(source * 2 + sib, part))

    gather_rows(pair_own, True)

    relay("+", "O0", prev, 0)
    onward("+", "F0", prev, 0)
    relay("-", "O2", nxt, 2)
    onward("-", "F0", nxt, 2)
    arrived("ty0", rim_after, has_after)
    arrived("ty1", rim_before, has_before)
    send("+H", piece(mp, "H"), peer(1, 0))
    send("-H", piece(mp, "H"), peer(-1, 0))
    send("2H", piece(mp, "H"), peer(2, 0))
    send("SH", piece(mp, "H"), peer(0, 1))
    for q in range(2):
        own_cols[q] = pack_row(pack_row(own_cols[q], q, -1), q, ROWS)
    send("tx0", own_cols, left, got_cols.at[0], has_left)
    to_right = copy("tx1", own_cols, got_cols.at[1], right)
    pl.when(greeted_right)(to_right.start)
    started.append((has_right, to_right))
    relay("+", "O1", prev, 1)
    onward("+", "F1", prev, 1)
    relay("-", "O3", nxt, 3)
    onward("-", "F1", nxt, 3)
    relay("+", "O2", prev, 2)
    relay("-", "O0", nxt, 0)
    relay("+", "O3", prev, 3)
    relay("-", "O1", nxt, 1)
    gather_rows([prev * 2 + core, nxt * 2 + core], False)
    relay("+", "H", prev, "H")
    relay("-", "H", nxt, "H")
    relay("2", "H", far, "H")
    relay("+", "F0", far, 0)
    relay("-", "F0", far, 2)
    def go_right():
        pl.semaphore_wait(leave, 1)
        to_right.start()

    pl.when(needs_leave)(go_right)
    arrived("tx0", got_cols.at[0], has_right)
    arrived("tx1", got_cols.at[1], has_left)
    for q in range(2):
        mine = own_cols[q]
        cols = jnp.where(lane < 64, pltpu.roll(got_cols[1, q], 32, 1), pltpu.roll(got_cols[0, q], 96, 1))
        held[mp, COLS + q] = jnp.where((lane < 32) | (lane >= 96), mine, cols)
    for a, b in peers:
        send("P%d%d" % (a, b), held.at[mp, pl.ds(COLS, 2)], peer(a, b))

    relay("+", "F1", far, 1)
    relay("-", "F1", far, 3)
    for k in range(4):
        from_sibling("+", "O%d" % k, prev, k)
        from_sibling("-", "O%d" % k, nxt, k)
    gather_rows([prev * 2 + sib, nxt * 2 + sib], False)

    alpha = coupling[mp]
    ratio = tv_weight[mp] / alpha

    def fluxes(m, g, e):
        size_sq = g[0] * g[0] + g[1] * g[1] + g[2] * g[2] + EPS_SQ
        tv = ratio * lax.rsqrt(size_sq)
        a00, a11, a22 = m[1] + m[2] + tv, m[0] + m[2] + tv, m[0] + m[1] + tv
        b00, b11, b22 = m[10] + m[14], m[6] + m[14], m[6] + m[10]
        q = (
            a00 * g[0] - (m[3] * g[1] + m[4] * g[2]),
            a11 * g[1] - (m[3] * g[0] + m[5] * g[2]),
            a22 * g[2] - (m[4] * g[0] + m[5] * g[1]),
        )
        p = (
            (a00 * e[0] + b00 * g[0]) - ((m[3] * e[1] + m[4] * e[2]) + (m[7] * g[1] + m[8] * g[2])),
            (a11 * e[1] + b11 * g[1]) - ((m[3] * e[0] + m[5] * e[2]) + (m[9] * g[0] + m[11] * g[2])),
            (a22 * e[2] + b22 * g[2]) - ((m[4] * e[0] + m[5] * e[1]) + (m[12] * g[0] + m[13] * g[1])),
        )
        return q, p

    def along_z(fz):
        fz = jnp.where(inner_z, fz, 0.0)
        return jnp.where(level == 0, 0.0, pltpu.roll(fz, 1, 0)) - fz

    outs = (gout, hout)

    def put_row(i, both, before_y, keep=None):
        new = []
        for q in range(2):
            fx, fy, fz = both[q]
            if keep is not None:
                fy = fy * keep
            enters = jnp.where(lane == 0, 0.0, pltpu.roll(fx, 1, 1))
            rest = jnp.where(lane == LANES - 1, 0.0, before_y[q] - fy + along_z(fz) - fx)
            outs[q][pl.ds(i - 1, NZ, stride=ROWS), :] = alpha * (enters + rest)
            new.append(fy)
        return tuple(new)

    for d, first in (("+", 0), ("-", 2)):
        from_sibling(d, "F0", far, first)
        from_sibling(d, "F1", far, first + 1)

    def out_body(i, carry):
        acc = row_moments([moms[i, j] for j in range(15)], pair_far, i)
        return put_row(i, fluxes(acc, *row_fields(mp, i)), carry)

    carry = lax.fori_loop(1, ROWS, out_body, (zero, zero), unroll=5)

    arrived("SH", piece(chip * 2 + sib, "H"))
    from_sibling("+", "H", prev, "H")
    from_sibling("-", "H", nxt, "H")
    from_sibling("2", "H", far, "H")
    every = range(MODELS)
    put_row(ROWS, fluxes(row_moments(None, every, ROWS), *row_fields(mp, ROWS)), carry, keep_last)
    keep_first = alpha * jnp.where(has_before, 1.0, 0.0)
    entering = [f[1] * keep_first for f in fluxes(row_moments(None, every, 0), *row_fields(mp, 0))]

    for a, b in peers:
        owner = at_chip(-a) * 2 + (sib if b else core)
        arrived("P%d%d" % (a, b), held.at[owner, pl.ds(COLS, 2)])
    no_x = (lane < 32) & (tx == n_tx - 1)
    no_y = ((lane == ROWS) | (lane == ROWS + 32)) & (ty == n_ty - 1)

    def col_fields(model):
        out = []
        for q in range(2):
            v = held[model, COLS + q]
            dx = jnp.where(no_x, 0.0, pltpu.roll(v, 64, 1) - v)
            dy = jnp.where(no_y, 0.0, pltpu.roll(v, LANES - 1, 1) - v)
            dz = jnp.where(inner_z, pltpu.roll(v, NZ - 1, 0) - v, 0.0)
            out.append((dx, dy, dz))
        return out

    col_moms = None
    for model in range(MODELS):
        g, e = col_fields(model)
        col_moms = add_moments(col_moms, g, e, coupling[model])
    off_x = no_x | ((lane >= 32) & (tx == 0))
    off_y = no_y | ((lane == 0) & (ty == 0))
    for q, f in enumerate(fluxes(col_moms, *col_fields(mp))):
        fx = jnp.where(off_x, 0.0, f[0])
        fy = jnp.where(off_y, 0.0, f[1])
        col_flux[0, q] = alpha * (pltpu.roll(fy, 1, 1) - fy + along_z(f[2]) - fx)
        col_flux[1, q] = alpha * fx
    for q in range(2):
        ends, starts = col_flux[0, q], col_flux[1, q]
        for r in range(ROWS):
            rows = pl.ds(r, NZ, stride=ROWS)
            more = jnp.where(lane == LANES - 1, pltpu.roll(ends, 126 - r, 1), 0.0)
            more = jnp.where(lane == 0, pltpu.roll(starts, 95 - r, 1), more)
            if r == 0:
                more = more + jnp.where(lane == LANES - 1, 0.0, entering[q])
            outs[q][rows, :] = outs[q][rows, :] + more

    for wanted, c in started:
        if wanted is None:
            c.wait_send()
        else:
            pl.when(wanted)(c.wait_send)


def shards(models, direction, coupling, tv_weight):
    flat = (NZ * ROWS, LANES)
    n = len(NAMES)
    out = pl.pallas_call(
        kernel,
        name="fused",
        out_shape=[pltpu.VMEM(flat, jnp.float32)] * 2,
        in_specs=[pl.BlockSpec(memory_space=pl.ANY)] * 4,
        out_specs=[pl.BlockSpec(memory_space=pltpu.VMEM)] * 2,
        scratch_shapes=[
            pltpu.VMEM((MODELS, SLABS, NZ, LANES), jnp.float32),
            pltpu.VMEM((2,) + flat, jnp.float32),
            pltpu.VMEM((ROWS + 1, 15, NZ, LANES), jnp.float32),
            pltpu.VMEM((2, NZ, LANES), jnp.float32),
            pltpu.VMEM((2, 2, NZ, LANES), jnp.float32),
            pltpu.VMEM((2, 2, NZ, LANES), jnp.float32),
            pltpu.SMEM((MODELS,), jnp.float32),
            pltpu.SMEM((MODELS,), jnp.float32),
            pltpu.SemaphoreType.DMA((4,)),
            pltpu.SemaphoreType.DMA((n,)),
            pltpu.SemaphoreType.DMA((n,)),
            pltpu.SemaphoreType.REGULAR,
        ],
        compiler_params=pltpu.CompilerParams(
            collective_id=1, has_side_effects=True, vmem_limit_bytes=60 * 2**20
        ),
    )(models.reshape(flat), direction.reshape(flat), coupling, tv_weight)
    return tuple(o.reshape(models.shape) for o in out)


def solution(mesh):
    placed = (P("mp", None, "ty", "tx"), P("mp", None, "ty", "tx"), P(), P())
    return jax.shard_map(
        shards,
        mesh=mesh,
        in_specs=placed,
        out_specs=(P("mp", None, "ty", "tx"), P("mp", None, "ty", "tx")),
        check_vma=False,
    )
```

```python
import functools

import jax
import jax.numpy as jnp
from jax import lax
from jax.experimental import pallas as pl
from jax.experimental.pallas import tpu as pltpu
from jax.sharding import PartitionSpec as P

EPS_SQ = 0.25
MESH = pl.DeviceIdType.MESH
MODELS = 8
CHIPS = 4
NZ = 16
ROWS = 16
LANES = 128
SLABS = 38
COLS = 36

RING = ("O0", "O1", "O2", "O3", "H", "F0", "F1")
NAMES = (
    ["ty0", "ty1", "tx0", "tx1", "S", "SH"]
    + [d + k for d in "+-" for k in RING] + ["2H"]
    + ["X" + d + k for d in "+-" for k in RING] + ["X2H"]
    + ["P%d%d" % (a, b) for a in range(CHIPS) for b in range(2) if a + b > 0]
)
INDEX = {name: i for i, name in enumerate(NAMES)}


def kernel(
    x_hbm, d_hbm, coupling_hbm, tv_hbm, outs,
    held, tile, moms, own_cols, got_cols, col_flux, coupling, tv_weight, in_sem, send_sem, recv_sem, leave,
):
    mp, tx, ty = (lax.axis_index(a) for a in ("mp", "tx", "ty"))
    n_tx, n_ty = lax.axis_size("tx"), lax.axis_size("ty")
    chip, core = mp // 2, mp % 2
    sib = 1 - core

    def at_chip(by):
        return lax.rem(chip + by + CHIPS, CHIPS)

    def peer(by, other):
        return (at_chip(by) * 2 + (sib if other else core), tx, ty)

    left, right = (mp, jnp.maximum(tx - 1, 0), ty), (mp, jnp.minimum(tx + 1, n_tx - 1), ty)
    before, after = (mp, tx, jnp.maximum(ty - 1, 0)), (mp, tx, jnp.minimum(ty + 1, n_ty - 1))
    has_left, has_right, has_before, has_after = tx > 0, tx < n_tx - 1, ty > 0, ty < n_ty - 1
    greets_left, greeted_right = tx == n_tx - 1, tx == n_tx - 2
    gives_leave = has_left & jnp.logical_not(greets_left)
    needs_leave = has_right & jnp.logical_not(greeted_right)
    peers = [(2, 0), (2, 1), (1, 0), (3, 0), (1, 1), (3, 1), (0, 1)]

    barrier = pltpu.get_barrier_semaphore()

    def greet(device):
        pl.semaphore_signal(barrier, inc=1, device_id=device, device_id_type=MESH)

    for wanted, device in ((has_before, before), (has_after, after), (has_right, right), (greets_left, left)):
        pl.when(wanted)(functools.partial(greet, device))
    for a, b in peers:
        greet(peer(a, b))
    loads = [
        pltpu.make_async_copy(src, dst, in_sem.at[i])
        for i, (src, dst) in enumerate(
            ((x_hbm, tile.at[0]), (d_hbm, tile.at[1]), (coupling_hbm, coupling), (tv_hbm, tv_weight))
        )
    ]
    for load in loads:
        load.start()

    lane = lax.broadcasted_iota(jnp.int32, (NZ, LANES), 1)
    level = lax.broadcasted_iota(jnp.int32, (NZ, LANES), 0)
    inner_z = level < NZ - 1
    zero = jnp.zeros((NZ, LANES), jnp.float32)

    started = []

    def copy(name, src, dst, device):
        i = INDEX[name]
        return pltpu.make_async_remote_copy(
            src_ref=src, dst_ref=dst, send_sem=send_sem.at[i], recv_sem=recv_sem.at[i],
            device_id=device, device_id_type=MESH,
        )

    def send(name, src, device, dst=None, wanted=None):
        c = copy(name, src, src if dst is None else dst, device)
        if wanted is None:
            c.start()
        else:
            pl.when(wanted)(c.start)
        started.append((wanted, c))

    def arrived(name, dst, wanted=None):
        wait = copy(name, dst, dst, peer(0, 1)).wait_recv
        if wanted is None:
            wait()
        else:
            pl.when(wanted)(wait)

    def piece(model, part):
        first, n = {"H": (0, 4), "all": (4, 32)}.get(part) or (4 + 8 * part, 8)
        return held.at[model, pl.ds(first, n)]

    def pack_row(cols, q, r):
        v = held[mp, 2 * ((r + 2) % 18) + q]
        low = pltpu.roll(v, (r + 2) % LANES, 1)
        high = pltpu.roll(v, (r + 97) % LANES, 1)
        cols = jnp.where(lane == r + 1, low, cols)
        return jnp.where(lane == r + 97, high, cols)

    def blank(ref):
        ref[...] = jnp.zeros(ref.shape, jnp.float32)

    rim_after, rim_before = held.at[mp, pl.ds(0, 2)], held.at[mp, pl.ds(2, 2)]
    for missing, ref in (
        (jnp.logical_not(has_after), rim_after), (jnp.logical_not(has_before), rim_before),
        (jnp.logical_not(has_right), got_cols.at[0]), (jnp.logical_not(has_left), got_cols.at[1]),
    ):
        pl.when(missing)(functools.partial(blank, ref))
    for load in loads:
        load.wait()
    for q in range(2):
        for r in range(ROWS):
            held[mp, 2 * (r + 2) + q] = tile[q, pl.ds(r, NZ, stride=ROWS), :]
    for q in range(2):
        cols = zero
        for r in range(ROWS):
            cols = pack_row(cols, q, r)
        own_cols[q] = cols

    expected = len(peers) + sum(w.astype(jnp.int32) for w in (has_before, has_after, has_left, greeted_right))
    pl.semaphore_wait(barrier, expected)

    send("ty0", held.at[mp, pl.ds(4, 2)], before, rim_after, has_before)
    send("ty1", held.at[mp, pl.ds(34, 2)], after, rim_before, has_after)
    for up, down in ((0, 2), (1, 3), (2, 0), (3, 1)):
        send("+O%d" % up, piece(mp, up), peer(1, 0))
        send("-O%d" % down, piece(mp, down), peer(-1, 0))
        if up == 1:
            send("S", piece(mp, "all"), peer(0, 1))

    def give_leave():
        pl.semaphore_signal(leave, inc=1, device_id=left, device_id_type=MESH)

    pl.when(gives_leave)(give_leave)
    arrived("S", piece(chip * 2 + sib, "all"))

    def differences(f, f_next, keep_y=None):
        dx = pltpu.roll(f, LANES - 1, 1) - f
        dy = f_next - f
        if keep_y is not None:
            dy = dy * keep_y
        dz = jnp.where(inner_z, pltpu.roll(f, NZ - 1, 0) - f, 0.0)
        return dx, dy, dz

    keep_last = jnp.where(has_after, 1.0, 0.0)

    def row_fields(model, i):
        here = 2 * (i + 1)
        last = isinstance(i, int) and i == ROWS
        then = 0 if last else 2 * (i + 2)
        keep = keep_last if last else None
        g = differences(held[model, here], held[model, then], keep)
        e = differences(held[model, here + 1], held[model, then + 1], keep)
        return g, e

    def add_moments(acc, g, e, weight):
        w = [weight * v for v in g]
        terms = [w[0] * g[0], w[1] * g[1], w[2] * g[2], w[0] * g[1], w[0] * g[2], w[1] * g[2]]
        terms += [e[i] * w[j] for i in range(3) for j in range(3)]
        return terms if acc is None else [a + t for a, t in zip(acc, terms)]

    def row_moments(acc, models, i):
        for model in models:
            g, e = row_fields(model, i)
            acc = add_moments(acc, g, e, coupling[model])
        return acc

    def gather_rows(models, fresh):
        def body(i, carry):
            acc = row_moments(None if fresh else [moms[i, j] for j in range(15)], models, i)
            for j in range(15):
                moms[i, j] = acc[j]
            return carry

        lax.fori_loop(1, ROWS, body, 0, unroll=5)

    prev, nxt, far = at_chip(-1), at_chip(1), at_chip(2)
    pair_own, pair_far = [chip * 2, chip * 2 + 1], [far * 2, far * 2 + 1]

    def relay(d, kind, source, part):
        ref = piece(source * 2 + core, part)
        arrived(d + kind, ref)
        send("X" + d + kind, ref, peer(0, 1))

    def onward(d, kind, source, part):
        send(d + kind, piece(source * 2 + core, part), peer(1 if d == "+" else -1, 0))

    def from_sibling(d, kind, source, part):
        arrived("X" + d + kind, piece(source * 2 + sib, part))

    gather_rows(pair_own, True)

    relay("+", "O0", prev, 0)
    onward("+", "F0", prev, 0)
    relay("-", "O2", nxt, 2)
    onward("-", "F0", nxt, 2)
    arrived("ty0", rim_after, has_after)
    arrived("ty1", rim_before, has_before)
    send("+H", piece(mp, "H"), peer(1, 0))
    send("-H", piece(mp, "H"), peer(-1, 0))
    send("2H", piece(mp, "H"), peer(2, 0))
    send("SH", piece(mp, "H"), peer(0, 1))
    for q in range(2):
        own_cols[q] = pack_row(pack_row(own_cols[q], q, -1), q, ROWS)
    send("tx0", own_cols, left, got_cols.at[0], has_left)
    to_right = copy("tx1", own_cols, got_cols.at[1], right)
    pl.when(greeted_right)(to_right.start)
    started.append((has_right, to_right))
    relay("+", "O1", prev, 1)
    onward("+", "F1", prev, 1)
    relay("-", "O3", nxt, 3)
    onward("-", "F1", nxt, 3)
    relay("+", "O2", prev, 2)
    relay("-", "O0", nxt, 0)
    relay("+", "O3", prev, 3)
    relay("-", "O1", nxt, 1)
    gather_rows([prev * 2 + core, nxt * 2 + core], False)
    relay("+", "H", prev, "H")
    relay("-", "H", nxt, "H")
    relay("2", "H", far, "H")
    relay("+", "F0", far, 0)
    relay("-", "F0", far, 2)
    def go_right():
        pl.semaphore_wait(leave, 1)
        to_right.start()

    pl.when(needs_leave)(go_right)
    arrived("tx0", got_cols.at[0], has_right)
    arrived("tx1", got_cols.at[1], has_left)
    for q in range(2):
        mine = own_cols[q]
        cols = jnp.where(lane < 64, pltpu.roll(got_cols[1, q], 32, 1), pltpu.roll(got_cols[0, q], 96, 1))
        held[mp, COLS + q] = jnp.where((lane < 32) | (lane >= 96), mine, cols)
    for a, b in peers:
        send("P%d%d" % (a, b), held.at[mp, pl.ds(COLS, 2)], peer(a, b))

    relay("+", "F1", far, 1)
    relay("-", "F1", far, 3)
    for k in range(4):
        from_sibling("+", "O%d" % k, prev, k)
        from_sibling("-", "O%d" % k, nxt, k)
    gather_rows([prev * 2 + sib, nxt * 2 + sib], False)

    alpha = coupling[mp]
    ratio = tv_weight[mp] / alpha

    def fluxes(m, g, e):
        size_sq = g[0] * g[0] + g[1] * g[1] + g[2] * g[2] + EPS_SQ
        tv = ratio * lax.rsqrt(size_sq)
        a00, a11, a22 = m[1] + m[2] + tv, m[0] + m[2] + tv, m[0] + m[1] + tv
        b00, b11, b22 = m[10] + m[14], m[6] + m[14], m[6] + m[10]
        q = (
            a00 * g[0] - (m[3] * g[1] + m[4] * g[2]),
            a11 * g[1] - (m[3] * g[0] + m[5] * g[2]),
            a22 * g[2] - (m[4] * g[0] + m[5] * g[1]),
        )
        p = (
            (a00 * e[0] + b00 * g[0]) - ((m[3] * e[1] + m[4] * e[2]) + (m[7] * g[1] + m[8] * g[2])),
            (a11 * e[1] + b11 * g[1]) - ((m[3] * e[0] + m[5] * e[2]) + (m[9] * g[0] + m[11] * g[2])),
            (a22 * e[2] + b22 * g[2]) - ((m[4] * e[0] + m[5] * e[1]) + (m[12] * g[0] + m[13] * g[1])),
        )
        return q, p

    def along_z(fz):
        fz = jnp.where(inner_z, fz, 0.0)
        return jnp.where(level == 0, 0.0, pltpu.roll(fz, 1, 0)) - fz

    def put_row(i, both, before_y, keep=None):
        new = []
        for q in range(2):
            fx, fy, fz = both[q]
            if keep is not None:
                fy = fy * keep
            enters = jnp.where(lane == 0, 0.0, pltpu.roll(fx, 1, 1))
            rest = jnp.where(lane == LANES - 1, 0.0, before_y[q] - fy + along_z(fz) - fx)
            outs[q, pl.ds(i - 1, NZ, stride=ROWS), :] = alpha * (enters + rest)
            new.append(fy)
        return tuple(new)

    for d, first in (("+", 0), ("-", 2)):
        from_sibling(d, "F0", far, first)
        from_sibling(d, "F1", far, first + 1)

    def out_body(i, carry):
        acc = row_moments([moms[i, j] for j in range(15)], pair_far, i)
        return put_row(i, fluxes(acc, *row_fields(mp, i)), carry)

    carry = lax.fori_loop(1, ROWS, out_body, (zero, zero), unroll=5)

    arrived("SH", piece(chip * 2 + sib, "H"))
    from_sibling("+", "H", prev, "H")
    from_sibling("-", "H", nxt, "H")
    from_sibling("2", "H", far, "H")
    every = range(MODELS)
    put_row(ROWS, fluxes(row_moments(None, every, ROWS), *row_fields(mp, ROWS)), carry, keep_last)
    keep_first = alpha * jnp.where(has_before, 1.0, 0.0)
    entering = [f[1] * keep_first for f in fluxes(row_moments(None, every, 0), *row_fields(mp, 0))]

    for wanted, c in started:
        if wanted is None:
            c.wait_send()
        else:
            pl.when(wanted)(c.wait_send)
    for a, b in peers:
        owner = at_chip(-a) * 2 + (sib if b else core)
        arrived("P%d%d" % (a, b), held.at[owner, pl.ds(COLS, 2)])
    no_x = (lane < 32) & (tx == n_tx - 1)
    no_y = ((lane == ROWS) | (lane == ROWS + 32)) & (ty == n_ty - 1)

    def col_fields(model):
        out = []
        for q in range(2):
            v = held[model, COLS + q]
            dx = jnp.where(no_x, 0.0, pltpu.roll(v, 64, 1) - v)
            dy = jnp.where(no_y, 0.0, pltpu.roll(v, LANES - 1, 1) - v)
            dz = jnp.where(inner_z, pltpu.roll(v, NZ - 1, 0) - v, 0.0)
            out.append((dx, dy, dz))
        return out

    col_moms = None
    for model in range(MODELS):
        g, e = col_fields(model)
        col_moms = add_moments(col_moms, g, e, coupling[model])
    off_x = no_x | ((lane >= 32) & (tx == 0))
    off_y = no_y | ((lane == 0) & (ty == 0))
    for q, f in enumerate(fluxes(col_moms, *col_fields(mp))):
        fx = jnp.where(off_x, 0.0, f[0])
        fy = jnp.where(off_y, 0.0, f[1])
        col_flux[0, q] = alpha * (pltpu.roll(fy, 1, 1) - fy + along_z(f[2]) - fx)
        col_flux[1, q] = alpha * fx
    for q in range(2):
        ends, starts = col_flux[0, q], col_flux[1, q]
        for r in range(ROWS):
            rows = pl.ds(r, NZ, stride=ROWS)
            more = jnp.where(lane == LANES - 1, pltpu.roll(ends, 126 - r, 1), 0.0)
            more = jnp.where(lane == 0, pltpu.roll(starts, 95 - r, 1), more)
            if r == 0:
                more = more + jnp.where(lane == LANES - 1, 0.0, entering[q])
            outs[q, rows, :] = outs[q, rows, :] + more


def shards(models, direction, coupling, tv_weight):
    flat = (NZ * ROWS, LANES)
    n = len(NAMES)
    out = pl.pallas_call(
        kernel,
        name="fused",
        out_shape=pltpu.VMEM((2,) + flat, jnp.float32),
        in_specs=[pl.BlockSpec(memory_space=pl.ANY)] * 4,
        out_specs=pl.BlockSpec(memory_space=pltpu.VMEM),
        scratch_shapes=[
            pltpu.VMEM((MODELS, SLABS, NZ, LANES), jnp.float32),
            pltpu.VMEM((2,) + flat, jnp.float32),
            pltpu.VMEM((ROWS + 1, 15, NZ, LANES), jnp.float32),
            pltpu.VMEM((2, NZ, LANES), jnp.float32),
            pltpu.VMEM((2, 2, NZ, LANES), jnp.float32),
            pltpu.VMEM((2, 2, NZ, LANES), jnp.float32),
            pltpu.SMEM((MODELS,), jnp.float32),
            pltpu.SMEM((MODELS,), jnp.float32),
            pltpu.SemaphoreType.DMA((4,)),
            pltpu.SemaphoreType.DMA((n,)),
            pltpu.SemaphoreType.DMA((n,)),
            pltpu.SemaphoreType.REGULAR,
        ],
        compiler_params=pltpu.CompilerParams(
            collective_id=1, has_side_effects=True, vmem_limit_bytes=60 * 2**20
        ),
    )(models.reshape(flat), direction.reshape(flat), coupling, tv_weight)
    return tuple(out[q].reshape(models.shape) for q in range(2))


def solution(mesh):
    placed = (P("mp", None, "ty", "tx"), P("mp", None, "ty", "tx"), P(), P())
    return jax.shard_map(
        shards,
        mesh=mesh,
        in_specs=placed,
        out_specs=(P("mp", None, "ty", "tx"), P("mp", None, "ty", "tx")),
        check_vma=False,
    )
```

```python
import functools

import jax
import jax.numpy as jnp
from jax import lax
from jax.experimental import pallas as pl
from jax.experimental.pallas import tpu as pltpu
from jax.sharding import PartitionSpec as P

EPS_SQ = 0.25
MESH = pl.DeviceIdType.MESH
MODELS = 8
CHIPS = 4
NZ = 16
ROWS = 16
LANES = 128
SLABS = 38
COLS = 36

RING = ("O0", "O1", "O2", "O3", "H", "F0", "F1")
NAMES = (
    ["ty0", "ty1", "tx0", "tx1", "S", "SH"]
    + [d + k for d in "+-" for k in RING] + ["2H"]
    + ["X" + d + k for d in "+-" for k in RING] + ["X2H"]
    + ["P%d%d" % (a, b) for a in range(CHIPS) for b in range(2) if a + b > 0]
)
INDEX = {name: i for i, name in enumerate(NAMES)}


def kernel(
    x_hbm, d_hbm, coupling_hbm, tv_hbm, outs,
    held, tile, moms, own_cols, got_cols, col_flux, coupling, tv_weight, in_sem, send_sem, recv_sem, leave,
):
    mp, tx, ty = (lax.axis_index(a) for a in ("mp", "tx", "ty"))
    n_tx, n_ty = lax.axis_size("tx"), lax.axis_size("ty")
    chip, core = mp // 2, mp % 2
    sib = 1 - core

    def at_chip(by):
        return lax.rem(chip + by + CHIPS, CHIPS)

    def peer(by, other):
        return (at_chip(by) * 2 + (sib if other else core), tx, ty)

    left, right = (mp, jnp.maximum(tx - 1, 0), ty), (mp, jnp.minimum(tx + 1, n_tx - 1), ty)
    before, after = (mp, tx, jnp.maximum(ty - 1, 0)), (mp, tx, jnp.minimum(ty + 1, n_ty - 1))
    has_left, has_right, has_before, has_after = tx > 0, tx < n_tx - 1, ty > 0, ty < n_ty - 1
    greets_left, greeted_right = tx == n_tx - 1, tx == n_tx - 2
    gives_leave = has_left & jnp.logical_not(greets_left)
    needs_leave = has_right & jnp.logical_not(greeted_right)
    peers = [(2, 0), (2, 1), (1, 0), (3, 0), (1, 1), (3, 1), (0, 1)]

    barrier = pltpu.get_barrier_semaphore()

    def greet(device):
        pl.semaphore_signal(barrier, inc=1, device_id=device, device_id_type=MESH)

    for wanted, device in ((has_before, before), (has_after, after), (has_right, right), (greets_left, left)):
        pl.when(wanted)(functools.partial(greet, device))
    for a, b in peers:
        greet(peer(a, b))
    loads = [
        pltpu.make_async_copy(src, dst, in_sem.at[i])
        for i, (src, dst) in enumerate(
            ((x_hbm, tile.at[0]), (d_hbm, tile.at[1]), (coupling_hbm, coupling), (tv_hbm, tv_weight))
        )
    ]
    for load in loads:
        load.start()

    lane = lax.broadcasted_iota(jnp.int32, (NZ, LANES), 1)
    level = lax.broadcasted_iota(jnp.int32, (NZ, LANES), 0)
    inner_z = level < NZ - 1
    zero = jnp.zeros((NZ, LANES), jnp.float32)

    started = []

    def copy(name, src, dst, device):
        i = INDEX[name]
        return pltpu.make_async_remote_copy(
            src_ref=src, dst_ref=dst, send_sem=send_sem.at[i], recv_sem=recv_sem.at[i],
            device_id=device, device_id_type=MESH,
        )

    def send(name, src, device, dst=None, wanted=None):
        c = copy(name, src, src if dst is None else dst, device)
        if wanted is None:
            c.start()
        else:
            pl.when(wanted)(c.start)
        started.append((wanted, c))

    def arrived(name, dst, wanted=None):
        wait = copy(name, dst, dst, peer(0, 1)).wait_recv
        if wanted is None:
            wait()
        else:
            pl.when(wanted)(wait)

    def piece(model, part):
        first, n = {"H": (0, 4), "all": (4, 32)}.get(part) or (4 + 8 * part, 8)
        return held.at[model, pl.ds(first, n)]

    def pack_row(cols, q, r):
        v = held[mp, 2 * ((r + 2) % 18) + q]
        low = pltpu.roll(v, (r + 2) % LANES, 1)
        high = pltpu.roll(v, (r + 97) % LANES, 1)
        cols = jnp.where(lane == r + 1, low, cols)
        return jnp.where(lane == r + 97, high, cols)

    def blank(ref):
        ref[...] = jnp.zeros(ref.shape, jnp.float32)

    rim_after, rim_before = held.at[mp, pl.ds(0, 2)], held.at[mp, pl.ds(2, 2)]
    for missing, ref in (
        (jnp.logical_not(has_after), rim_after), (jnp.logical_not(has_before), rim_before),
        (jnp.logical_not(has_right), got_cols.at[0]), (jnp.logical_not(has_left), got_cols.at[1]),
    ):
        pl.when(missing)(functools.partial(blank, ref))
    for load in loads:
        load.wait()
    for q in range(2):
        for r in range(ROWS):
            held[mp, 2 * (r + 2) + q] = tile[q, pl.ds(r, NZ, stride=ROWS), :]
    for q in range(2):
        cols = zero
        for r in range(ROWS):
            cols = pack_row(cols, q, r)
        own_cols[q] = cols

    expected = len(peers) + sum(w.astype(jnp.int32) for w in (has_before, has_after, has_left, greeted_right))
    pl.semaphore_wait(barrier, expected)

    send("ty0", held.at[mp, pl.ds(4, 2)], before, rim_after, has_before)
    send("ty1", held.at[mp, pl.ds(34, 2)], after, rim_before, has_after)
    for up, down in ((0, 2), (1, 3), (2, 0), (3, 1)):
        send("+O%d" % up, piece(mp, up), peer(1, 0))
        send("-O%d" % down, piece(mp, down), peer(-1, 0))
        if up == 1:
            send("S", piece(mp, "all"), peer(0, 1))

    def give_leave():
        pl.semaphore_signal(leave, inc=1, device_id=left, device_id_type=MESH)

    pl.when(gives_leave)(give_leave)
    def differences(f, f_next, keep_y=None):
        dx = pltpu.roll(f, LANES - 1, 1) - f
        dy = f_next - f
        if keep_y is not None:
            dy = dy * keep_y
        dz = jnp.where(inner_z, pltpu.roll(f, NZ - 1, 0) - f, 0.0)
        return dx, dy, dz

    keep_last = jnp.where(has_after, 1.0, 0.0)

    def row_fields(model, i):
        here = 2 * (i + 1)
        last = isinstance(i, int) and i == ROWS
        then = 0 if last else 2 * (i + 2)
        keep = keep_last if last else None
        g = differences(held[model, here], held[model, then], keep)
        e = differences(held[model, here + 1], held[model, then + 1], keep)
        return g, e

    def add_moments(acc, g, e, weight):
        w = [weight * v for v in g]
        terms = [w[0] * g[0], w[1] * g[1], w[2] * g[2], w[0] * g[1], w[0] * g[2], w[1] * g[2]]
        terms += [e[i] * w[j] for i in range(3) for j in range(3)]
        return terms if acc is None else [a + t for a, t in zip(acc, terms)]

    def row_moments(acc, models, i):
        for model in models:
            g, e = row_fields(model, i)
            acc = add_moments(acc, g, e, coupling[model])
        return acc

    def gather_rows(models, fresh):
        def body(i, carry):
            acc = row_moments(None if fresh else [moms[i, j] for j in range(15)], models, i)
            for j in range(15):
                moms[i, j] = acc[j]
            return carry

        lax.fori_loop(1, ROWS, body, 0, unroll=5)

    prev, nxt, far = at_chip(-1), at_chip(1), at_chip(2)
    pair_own, pair_far = [chip * 2, chip * 2 + 1], [far * 2, far * 2 + 1]

    def relay(d, kind, source, part):
        ref = piece(source * 2 + core, part)
        arrived(d + kind, ref)
        send("X" + d + kind, ref, peer(0, 1))

    def onward(d, kind, source, part):
        send(d + kind, piece(source * 2 + core, part), peer(1 if d == "+" else -1, 0))

    def from_sibling(d, kind, source, part):
        arrived("X" + d + kind, piece(source * 2 + sib, part))

    arrived("ty0", rim_after, has_after)
    arrived("ty1", rim_before, has_before)
    for q in range(2):
        own_cols[q] = pack_row(pack_row(own_cols[q], q, -1), q, ROWS)
    send("tx0", own_cols, left, got_cols.at[0], has_left)
    to_right = copy("tx1", own_cols, got_cols.at[1], right)
    pl.when(greeted_right)(to_right.start)
    started.append((has_right, to_right))
    relay("+", "O0", prev, 0)
    onward("+", "F0", prev, 0)
    relay("-", "O2", nxt, 2)
    onward("-", "F0", nxt, 2)
    send("+H", piece(mp, "H"), peer(1, 0))
    send("-H", piece(mp, "H"), peer(-1, 0))
    send("2H", piece(mp, "H"), peer(2, 0))
    send("SH", piece(mp, "H"), peer(0, 1))
    relay("+", "O1", prev, 1)
    onward("+", "F1", prev, 1)
    relay("-", "O3", nxt, 3)
    onward("-", "F1", nxt, 3)
    arrived("S", piece(chip * 2 + sib, "all"))
    gather_rows(pair_own, True)
    relay("+", "O2", prev, 2)
    relay("-", "O0", nxt, 0)
    relay("+", "O3", prev, 3)
    relay("-", "O1", nxt, 1)
    gather_rows([prev * 2 + core, nxt * 2 + core], False)
    relay("+", "H", prev, "H")
    relay("-", "H", nxt, "H")
    relay("2", "H", far, "H")
    relay("+", "F0", far, 0)
    relay("-", "F0", far, 2)
    def go_right():
        pl.semaphore_wait(leave, 1)
        to_right.start()

    pl.when(needs_leave)(go_right)
    arrived("tx0", got_cols.at[0], has_right)
    arrived("tx1", got_cols.at[1], has_left)
    for q in range(2):
        mine = own_cols[q]
        cols = jnp.where(lane < 64, pltpu.roll(got_cols[1, q], 32, 1), pltpu.roll(got_cols[0, q], 96, 1))
        held[mp, COLS + q] = jnp.where((lane < 32) | (lane >= 96), mine, cols)
    for a, b in peers:
        send("P%d%d" % (a, b), held.at[mp, pl.ds(COLS, 2)], peer(a, b))

    relay("+", "F1", far, 1)
    relay("-", "F1", far, 3)
    for k in range(4):
        from_sibling("+", "O%d" % k, prev, k)
        from_sibling("-", "O%d" % k, nxt, k)
    gather_rows([prev * 2 + sib, nxt * 2 + sib], False)

    alpha = coupling[mp]
    ratio = tv_weight[mp] / alpha

    def fluxes(m, g, e):
        size_sq = g[0] * g[0] + g[1] * g[1] + g[2] * g[2] + EPS_SQ
        tv = ratio * lax.rsqrt(size_sq)
        a00, a11, a22 = m[1] + m[2] + tv, m[0] + m[2] + tv, m[0] + m[1] + tv
        b00, b11, b22 = m[10] + m[14], m[6] + m[14], m[6] + m[10]
        q = (
            a00 * g[0] - (m[3] * g[1] + m[4] * g[2]),
            a11 * g[1] - (m[3] * g[0] + m[5] * g[2]),
            a22 * g[2] - (m[4] * g[0] + m[5] * g[1]),
        )
        p = (
            (a00 * e[0] + b00 * g[0]) - ((m[3] * e[1] + m[4] * e[2]) + (m[7] * g[1] + m[8] * g[2])),
            (a11 * e[1] + b11 * g[1]) - ((m[3] * e[0] + m[5] * e[2]) + (m[9] * g[0] + m[11] * g[2])),
            (a22 * e[2] + b22 * g[2]) - ((m[4] * e[0] + m[5] * e[1]) + (m[12] * g[0] + m[13] * g[1])),
        )
        return q, p

    def along_z(fz):
        fz = jnp.where(inner_z, fz, 0.0)
        return jnp.where(level == 0, 0.0, pltpu.roll(fz, 1, 0)) - fz

    def put_row(i, both, before_y, keep=None):
        new = []
        for q in range(2):
            fx, fy, fz = both[q]
            if keep is not None:
                fy = fy * keep
            enters = jnp.where(lane == 0, 0.0, pltpu.roll(fx, 1, 1))
            rest = jnp.where(lane == LANES - 1, 0.0, before_y[q] - fy + along_z(fz) - fx)
            outs[q, pl.ds(i - 1, NZ, stride=ROWS), :] = alpha * (enters + rest)
            new.append(fy)
        return tuple(new)

    for d, first in (("+", 0), ("-", 2)):
        from_sibling(d, "F0", far, first)
        from_sibling(d, "F1", far, first + 1)

    def out_body(i, carry):
        acc = row_moments([moms[i, j] for j in range(15)], pair_far, i)
        return put_row(i, fluxes(acc, *row_fields(mp, i)), carry)

    carry = lax.fori_loop(1, ROWS, out_body, (zero, zero), unroll=5)

    arrived("SH", piece(chip * 2 + sib, "H"))
    from_sibling("+", "H", prev, "H")
    from_sibling("-", "H", nxt, "H")
    from_sibling("2", "H", far, "H")
    every = range(MODELS)
    put_row(ROWS, fluxes(row_moments(None, every, ROWS), *row_fields(mp, ROWS)), carry, keep_last)
    keep_first = alpha * jnp.where(has_before, 1.0, 0.0)
    entering = [f[1] * keep_first for f in fluxes(row_moments(None, every, 0), *row_fields(mp, 0))]

    for wanted, c in started:
        if wanted is None:
            c.wait_send()
        else:
            pl.when(wanted)(c.wait_send)
    for a, b in peers:
        owner = at_chip(-a) * 2 + (sib if b else core)
        arrived("P%d%d" % (a, b), held.at[owner, pl.ds(COLS, 2)])
    no_x = (lane < 32) & (tx == n_tx - 1)
    no_y = ((lane == ROWS) | (lane == ROWS + 32)) & (ty == n_ty - 1)

    def col_fields(model):
        out = []
        for q in range(2):
            v = held[model, COLS + q]
            dx = jnp.where(no_x, 0.0, pltpu.roll(v, 64, 1) - v)
            dy = jnp.where(no_y, 0.0, pltpu.roll(v, LANES - 1, 1) - v)
            dz = jnp.where(inner_z, pltpu.roll(v, NZ - 1, 0) - v, 0.0)
            out.append((dx, dy, dz))
        return out

    col_moms = None
    for model in range(MODELS):
        g, e = col_fields(model)
        col_moms = add_moments(col_moms, g, e, coupling[model])
    off_x = no_x | ((lane >= 32) & (tx == 0))
    off_y = no_y | ((lane == 0) & (ty == 0))
    for q, f in enumerate(fluxes(col_moms, *col_fields(mp))):
        fx = jnp.where(off_x, 0.0, f[0])
        fy = jnp.where(off_y, 0.0, f[1])
        col_flux[0, q] = alpha * (pltpu.roll(fy, 1, 1) - fy + along_z(f[2]) - fx)
        col_flux[1, q] = alpha * fx
    for q in range(2):
        ends, starts = col_flux[0, q], col_flux[1, q]
        for r in range(ROWS):
            rows = pl.ds(r, NZ, stride=ROWS)
            more = jnp.where(lane == LANES - 1, pltpu.roll(ends, 126 - r, 1), 0.0)
            more = jnp.where(lane == 0, pltpu.roll(starts, 95 - r, 1), more)
            if r == 0:
                more = more + jnp.where(lane == LANES - 1, 0.0, entering[q])
            outs[q, rows, :] = outs[q, rows, :] + more


def shards(models, direction, coupling, tv_weight):
    flat = (NZ * ROWS, LANES)
    n = len(NAMES)
    out = pl.pallas_call(
        kernel,
        name="fused",
        out_shape=pltpu.VMEM((2,) + flat, jnp.float32),
        in_specs=[pl.BlockSpec(memory_space=pl.ANY)] * 4,
        out_specs=pl.BlockSpec(memory_space=pltpu.VMEM),
        scratch_shapes=[
            pltpu.VMEM((MODELS, SLABS, NZ, LANES), jnp.float32),
            pltpu.VMEM((2,) + flat, jnp.float32),
            pltpu.VMEM((ROWS + 1, 15, NZ, LANES), jnp.float32),
            pltpu.VMEM((2, NZ, LANES), jnp.float32),
            pltpu.VMEM((2, 2, NZ, LANES), jnp.float32),
            pltpu.VMEM((2, 2, NZ, LANES), jnp.float32),
            pltpu.SMEM((MODELS,), jnp.float32),
            pltpu.SMEM((MODELS,), jnp.float32),
            pltpu.SemaphoreType.DMA((4,)),
            pltpu.SemaphoreType.DMA((n,)),
            pltpu.SemaphoreType.DMA((n,)),
            pltpu.SemaphoreType.REGULAR,
        ],
        compiler_params=pltpu.CompilerParams(
            collective_id=1, has_side_effects=True, vmem_limit_bytes=60 * 2**20
        ),
    )(models.reshape(flat), direction.reshape(flat), coupling, tv_weight)
    return tuple(out[q].reshape(models.shape) for q in range(2))


def solution(mesh):
    placed = (P("mp", None, "ty", "tx"), P("mp", None, "ty", "tx"), P(), P())
    return jax.shard_map(
        shards,
        mesh=mesh,
        in_specs=placed,
        out_specs=(P("mp", None, "ty", "tx"), P("mp", None, "ty", "tx")),
        check_vma=False,
    )
```

```python
import functools

import jax
import jax.numpy as jnp
from jax import lax
from jax.experimental import pallas as pl
from jax.experimental.pallas import tpu as pltpu
from jax.sharding import PartitionSpec as P

EPS_SQ = 0.25
MESH = pl.DeviceIdType.MESH
MODELS = 8
CHIPS = 4
NZ = 16
ROWS = 16
LANES = 128
SLABS = 38
COLS = 36

RING = ("O0", "O1", "O2", "O3", "H", "F0", "F1")
NAMES = (
    ["ty0", "ty1", "tx0", "tx1", "S", "SH"]
    + [d + k for d in "+-" for k in RING] + ["2H"]
    + ["X" + d + k for d in "+-" for k in RING] + ["X2H"]
    + ["P%d%d" % (a, b) for a in range(CHIPS) for b in range(2) if a + b > 0]
)
INDEX = {name: i for i, name in enumerate(NAMES)}


def kernel(
    x_hbm, d_hbm, coupling_hbm, tv_hbm, outs,
    held, tile, moms, own_cols, got_cols, col_flux, coupling, tv_weight, in_sem, send_sem, recv_sem, leave,
):
    mp, tx, ty = (lax.axis_index(a) for a in ("mp", "tx", "ty"))
    n_tx, n_ty = lax.axis_size("tx"), lax.axis_size("ty")
    chip, core = mp // 2, mp % 2
    sib = 1 - core

    def at_chip(by):
        return lax.rem(chip + by + CHIPS, CHIPS)

    def peer(by, other):
        return (at_chip(by) * 2 + (sib if other else core), tx, ty)

    left, right = (mp, jnp.maximum(tx - 1, 0), ty), (mp, jnp.minimum(tx + 1, n_tx - 1), ty)
    before, after = (mp, tx, jnp.maximum(ty - 1, 0)), (mp, tx, jnp.minimum(ty + 1, n_ty - 1))
    has_left, has_right, has_before, has_after = tx > 0, tx < n_tx - 1, ty > 0, ty < n_ty - 1
    greets_left, greeted_right = tx == n_tx - 1, tx == n_tx - 2
    gives_leave = has_left & jnp.logical_not(greets_left)
    needs_leave = has_right & jnp.logical_not(greeted_right)
    peers = [(2, 0), (2, 1), (1, 0), (3, 0), (1, 1), (3, 1), (0, 1)]

    barrier = pltpu.get_barrier_semaphore()

    def greet(device):
        pl.semaphore_signal(barrier, inc=1, device_id=device, device_id_type=MESH)

    for wanted, device in ((has_before, before), (has_after, after), (has_right, right), (greets_left, left)):
        pl.when(wanted)(functools.partial(greet, device))
    for a, b in peers:
        greet(peer(a, b))
    loads = [
        pltpu.make_async_copy(src, dst, in_sem.at[i])
        for i, (src, dst) in enumerate(
            ((x_hbm, tile.at[0]), (d_hbm, tile.at[1]), (coupling_hbm, coupling), (tv_hbm, tv_weight))
        )
    ]
    for load in loads:
        load.start()

    lane = lax.broadcasted_iota(jnp.int32, (NZ, LANES), 1)
    level = lax.broadcasted_iota(jnp.int32, (NZ, LANES), 0)
    inner_z = level < NZ - 1
    zero = jnp.zeros((NZ, LANES), jnp.float32)

    started = []

    def copy(name, src, dst, device):
        i = INDEX[name]
        return pltpu.make_async_remote_copy(
            src_ref=src, dst_ref=dst, send_sem=send_sem.at[i], recv_sem=recv_sem.at[i],
            device_id=device, device_id_type=MESH,
        )

    def send(name, src, device, dst=None, wanted=None):
        c = copy(name, src, src if dst is None else dst, device)
        if wanted is None:
            c.start()
        else:
            pl.when(wanted)(c.start)
        started.append((wanted, c))

    def arrived(name, dst, wanted=None):
        wait = copy(name, dst, dst, peer(0, 1)).wait_recv
        if wanted is None:
            wait()
        else:
            pl.when(wanted)(wait)

    def piece(model, part):
        first, n = {"H": (0, 4), "all": (4, 32)}.get(part) or (4 + 8 * part, 8)
        return held.at[model, pl.ds(first, n)]

    def pack_row(cols, q, r):
        v = held[mp, 2 * ((r + 2) % 18) + q]
        low = pltpu.roll(v, (r + 2) % LANES, 1)
        high = pltpu.roll(v, (r + 97) % LANES, 1)
        cols = jnp.where(lane == r + 1, low, cols)
        return jnp.where(lane == r + 97, high, cols)

    def blank(ref):
        ref[...] = jnp.zeros(ref.shape, jnp.float32)

    rim_after, rim_before = held.at[mp, pl.ds(0, 2)], held.at[mp, pl.ds(2, 2)]
    for missing, ref in (
        (jnp.logical_not(has_after), rim_after), (jnp.logical_not(has_before), rim_before),
        (jnp.logical_not(has_right), got_cols.at[0]), (jnp.logical_not(has_left), got_cols.at[1]),
    ):
        pl.when(missing)(functools.partial(blank, ref))
    for load in loads:
        load.wait()
    for q in range(2):
        for r in range(ROWS):
            held[mp, 2 * (r + 2) + q] = tile[q, pl.ds(r, NZ, stride=ROWS), :]
    for q in range(2):
        cols = zero
        for r in range(ROWS):
            cols = pack_row(cols, q, r)
        own_cols[q] = cols

    expected = len(peers) + sum(w.astype(jnp.int32) for w in (has_before, has_after, has_left, greeted_right))
    pl.semaphore_wait(barrier, expected)

    send("ty0", held.at[mp, pl.ds(4, 2)], before, rim_after, has_before)
    send("ty1", held.at[mp, pl.ds(34, 2)], after, rim_before, has_after)
    for up, down in ((0, 2), (1, 3), (2, 0), (3, 1)):
        send("+O%d" % up, piece(mp, up), peer(1, 0))
        send("-O%d" % down, piece(mp, down), peer(-1, 0))
        if up == 1:
            send("S", piece(mp, "all"), peer(0, 1))

    def give_leave():
        pl.semaphore_signal(leave, inc=1, device_id=left, device_id_type=MESH)

    pl.when(gives_leave)(give_leave)
    def differences(f, f_next, keep_y=None):
        dx = pltpu.roll(f, LANES - 1, 1) - f
        dy = f_next - f
        if keep_y is not None:
            dy = dy * keep_y
        dz = jnp.where(inner_z, pltpu.roll(f, NZ - 1, 0) - f, 0.0)
        return dx, dy, dz

    keep_last = jnp.where(has_after, 1.0, 0.0)

    def row_fields(model, i):
        here = 2 * (i + 1)
        last = isinstance(i, int) and i == ROWS
        then = 0 if last else 2 * (i + 2)
        keep = keep_last if last else None
        g = differences(held[model, here], held[model, then], keep)
        e = differences(held[model, here + 1], held[model, then + 1], keep)
        return g, e

    def add_moments(acc, g, e, weight):
        w = [weight * v for v in g]
        terms = [w[0] * g[0], w[1] * g[1], w[2] * g[2], w[0] * g[1], w[0] * g[2], w[1] * g[2]]
        terms += [e[i] * w[j] for i in range(3) for j in range(3)]
        return terms if acc is None else [a + t for a, t in zip(acc, terms)]

    def row_moments(acc, models, i):
        for model in models:
            g, e = row_fields(model, i)
            acc = add_moments(acc, g, e, coupling[model])
        return acc

    def gather_rows(models, fresh):
        def body(i, carry):
            acc = row_moments(None if fresh else [moms[i, j] for j in range(15)], models, i)
            for j in range(15):
                moms[i, j] = acc[j]
            return carry

        lax.fori_loop(1, ROWS, body, 0, unroll=5)

    prev, nxt, far = at_chip(-1), at_chip(1), at_chip(2)
    pair_own, pair_far = [chip * 2, chip * 2 + 1], [far * 2, far * 2 + 1]

    def relay(d, kind, source, part):
        ref = piece(source * 2 + core, part)
        arrived(d + kind, ref)
        send("X" + d + kind, ref, peer(0, 1))

    def onward(d, kind, source, part):
        send(d + kind, piece(source * 2 + core, part), peer(1 if d == "+" else -1, 0))

    def from_sibling(d, kind, source, part):
        arrived("X" + d + kind, piece(source * 2 + sib, part))

    arrived("ty0", rim_after, has_after)
    arrived("ty1", rim_before, has_before)
    for q in range(2):
        own_cols[q] = pack_row(pack_row(own_cols[q], q, -1), q, ROWS)
    send("tx0", own_cols, left, got_cols.at[0], has_left)
    to_right = copy("tx1", own_cols, got_cols.at[1], right)
    pl.when(greeted_right)(to_right.start)
    started.append((has_right, to_right))
    relay("+", "O0", prev, 0)
    onward("+", "F0", prev, 0)
    relay("-", "O2", nxt, 2)
    onward("-", "F0", nxt, 2)
    relay("+", "O1", prev, 1)
    onward("+", "F1", prev, 1)
    relay("-", "O3", nxt, 3)
    onward("-", "F1", nxt, 3)
    send("+H", piece(mp, "H"), peer(1, 0))
    send("-H", piece(mp, "H"), peer(-1, 0))
    send("2H", piece(mp, "H"), peer(2, 0))
    send("SH", piece(mp, "H"), peer(0, 1))
    arrived("S", piece(chip * 2 + sib, "all"))
    gather_rows(pair_own, True)
    relay("+", "O2", prev, 2)
    relay("-", "O0", nxt, 0)
    relay("+", "O3", prev, 3)
    relay("-", "O1", nxt, 1)
    gather_rows([prev * 2 + core, nxt * 2 + core], False)
    relay("+", "F0", far, 0)
    relay("-", "F0", far, 2)

    def go_right():
        pl.semaphore_wait(leave, 1)
        to_right.start()

    pl.when(needs_leave)(go_right)
    arrived("tx0", got_cols.at[0], has_right)
    arrived("tx1", got_cols.at[1], has_left)
    for q in range(2):
        mine = own_cols[q]
        cols = jnp.where(lane < 64, pltpu.roll(got_cols[1, q], 32, 1), pltpu.roll(got_cols[0, q], 96, 1))
        held[mp, COLS + q] = jnp.where((lane < 32) | (lane >= 96), mine, cols)
    for a, b in peers:
        send("P%d%d" % (a, b), held.at[mp, pl.ds(COLS, 2)], peer(a, b))

    relay("+", "F1", far, 1)
    relay("-", "F1", far, 3)
    relay("+", "H", prev, "H")
    relay("-", "H", nxt, "H")
    relay("2", "H", far, "H")
    for k in range(4):
        from_sibling("+", "O%d" % k, prev, k)
        from_sibling("-", "O%d" % k, nxt, k)
    gather_rows([prev * 2 + sib, nxt * 2 + sib], False)

    alpha = coupling[mp]
    ratio = tv_weight[mp] / alpha

    def fluxes(m, g, e):
        size_sq = g[0] * g[0] + g[1] * g[1] + g[2] * g[2] + EPS_SQ
        tv = ratio * lax.rsqrt(size_sq)
        a00, a11, a22 = m[1] + m[2] + tv, m[0] + m[2] + tv, m[0] + m[1] + tv
        b00, b11, b22 = m[10] + m[14], m[6] + m[14], m[6] + m[10]
        q = (
            a00 * g[0] - (m[3] * g[1] + m[4] * g[2]),
            a11 * g[1] - (m[3] * g[0] + m[5] * g[2]),
            a22 * g[2] - (m[4] * g[0] + m[5] * g[1]),
        )
        p = (
            (a00 * e[0] + b00 * g[0]) - ((m[3] * e[1] + m[4] * e[2]) + (m[7] * g[1] + m[8] * g[2])),
            (a11 * e[1] + b11 * g[1]) - ((m[3] * e[0] + m[5] * e[2]) + (m[9] * g[0] + m[11] * g[2])),
            (a22 * e[2] + b22 * g[2]) - ((m[4] * e[0] + m[5] * e[1]) + (m[12] * g[0] + m[13] * g[1])),
        )
        return q, p

    def along_z(fz):
        fz = jnp.where(inner_z, fz, 0.0)
        return jnp.where(level == 0, 0.0, pltpu.roll(fz, 1, 0)) - fz

    def put_row(i, both, before_y, keep=None):
        new = []
        for q in range(2):
            fx, fy, fz = both[q]
            if keep is not None:
                fy = fy * keep
            enters = jnp.where(lane == 0, 0.0, pltpu.roll(fx, 1, 1))
            rest = jnp.where(lane == LANES - 1, 0.0, before_y[q] - fy + along_z(fz) - fx)
            outs[q, pl.ds(i - 1, NZ, stride=ROWS), :] = alpha * (enters + rest)
            new.append(fy)
        return tuple(new)

    for d, first in (("+", 0), ("-", 2)):
        from_sibling(d, "F0", far, first)
        from_sibling(d, "F1", far, first + 1)

    def out_body(i, carry):
        acc = row_moments([moms[i, j] for j in range(15)], pair_far, i)
        return put_row(i, fluxes(acc, *row_fields(mp, i)), carry)

    carry = lax.fori_loop(1, ROWS, out_body, (zero, zero), unroll=5)

    arrived("SH", piece(chip * 2 + sib, "H"))
    from_sibling("+", "H", prev, "H")
    from_sibling("-", "H", nxt, "H")
    from_sibling("2", "H", far, "H")
    every = range(MODELS)
    put_row(ROWS, fluxes(row_moments(None, every, ROWS), *row_fields(mp, ROWS)), carry, keep_last)
    keep_first = alpha * jnp.where(has_before, 1.0, 0.0)
    entering = [f[1] * keep_first for f in fluxes(row_moments(None, every, 0), *row_fields(mp, 0))]

    for wanted, c in started:
        if wanted is None:
            c.wait_send()
        else:
            pl.when(wanted)(c.wait_send)
    for a, b in peers:
        owner = at_chip(-a) * 2 + (sib if b else core)
        arrived("P%d%d" % (a, b), held.at[owner, pl.ds(COLS, 2)])
    no_x = (lane < 32) & (tx == n_tx - 1)
    no_y = ((lane == ROWS) | (lane == ROWS + 32)) & (ty == n_ty - 1)

    def col_fields(model):
        out = []
        for q in range(2):
            v = held[model, COLS + q]
            dx = jnp.where(no_x, 0.0, pltpu.roll(v, 64, 1) - v)
            dy = jnp.where(no_y, 0.0, pltpu.roll(v, LANES - 1, 1) - v)
            dz = jnp.where(inner_z, pltpu.roll(v, NZ - 1, 0) - v, 0.0)
            out.append((dx, dy, dz))
        return out

    col_moms = None
    for model in range(MODELS):
        g, e = col_fields(model)
        col_moms = add_moments(col_moms, g, e, coupling[model])
    off_x = no_x | ((lane >= 32) & (tx == 0))
    off_y = no_y | ((lane == 0) & (ty == 0))
    for q, f in enumerate(fluxes(col_moms, *col_fields(mp))):
        fx = jnp.where(off_x, 0.0, f[0])
        fy = jnp.where(off_y, 0.0, f[1])
        col_flux[0, q] = alpha * (pltpu.roll(fy, 1, 1) - fy + along_z(f[2]) - fx)
        col_flux[1, q] = alpha * fx
    for q in range(2):
        ends, starts = col_flux[0, q], col_flux[1, q]
        for r in range(ROWS):
            rows = pl.ds(r, NZ, stride=ROWS)
            more = jnp.where(lane == LANES - 1, pltpu.roll(ends, 126 - r, 1), 0.0)
            more = jnp.where(lane == 0, pltpu.roll(starts, 95 - r, 1), more)
            if r == 0:
                more = more + jnp.where(lane == LANES - 1, 0.0, entering[q])
            outs[q, rows, :] = outs[q, rows, :] + more


def shards(models, direction, coupling, tv_weight):
    flat = (NZ * ROWS, LANES)
    n = len(NAMES)
    out = pl.pallas_call(
        kernel,
        name="fused",
        out_shape=pltpu.VMEM((2,) + flat, jnp.float32),
        in_specs=[pl.BlockSpec(memory_space=pl.ANY)] * 4,
        out_specs=pl.BlockSpec(memory_space=pltpu.VMEM),
        scratch_shapes=[
            pltpu.VMEM((MODELS, SLABS, NZ, LANES), jnp.float32),
            pltpu.VMEM((2,) + flat, jnp.float32),
            pltpu.VMEM((ROWS + 1, 15, NZ, LANES), jnp.float32),
            pltpu.VMEM((2, NZ, LANES), jnp.float32),
            pltpu.VMEM((2, 2, NZ, LANES), jnp.float32),
            pltpu.VMEM((2, 2, NZ, LANES), jnp.float32),
            pltpu.SMEM((MODELS,), jnp.float32),
            pltpu.SMEM((MODELS,), jnp.float32),
            pltpu.SemaphoreType.DMA((4,)),
            pltpu.SemaphoreType.DMA((n,)),
            pltpu.SemaphoreType.DMA((n,)),
            pltpu.SemaphoreType.REGULAR,
        ],
        compiler_params=pltpu.CompilerParams(
            collective_id=1, has_side_effects=True, vmem_limit_bytes=60 * 2**20
        ),
    )(models.reshape(flat), direction.reshape(flat), coupling, tv_weight)
    return tuple(out[q].reshape(models.shape) for q in range(2))


def solution(mesh):
    placed = (P("mp", None, "ty", "tx"), P("mp", None, "ty", "tx"), P(), P())
    return jax.shard_map(
        shards,
        mesh=mesh,
        in_specs=placed,
        out_specs=(P("mp", None, "ty", "tx"), P("mp", None, "ty", "tx")),
        check_vma=False,
    )
```

```python
import functools

import jax
import jax.numpy as jnp
from jax import lax
from jax.experimental import pallas as pl
from jax.experimental.pallas import tpu as pltpu
from jax.sharding import PartitionSpec as P

EPS_SQ = 0.25
MESH = pl.DeviceIdType.MESH
MODELS = 8
CHIPS = 4
NZ = 16
ROWS = 16
LANES = 128
SLABS = 38
COLS = 36

RING = ("O0", "O1", "O2", "O3", "H", "F0", "F1")
NAMES = (
    ["ty0", "ty1", "tx0", "tx1", "S", "SH"]
    + [d + k for d in "+-" for k in RING] + ["2H"]
    + ["X" + d + k for d in "+-" for k in RING] + ["X2H"]
    + ["P%d%d" % (a, b) for a in range(CHIPS) for b in range(2) if a + b > 0]
)
INDEX = {name: i for i, name in enumerate(NAMES)}


def kernel(
    x_hbm, d_hbm, coupling_hbm, tv_hbm, outs,
    held, tile, moms, own_cols, got_cols, col_flux, coupling, tv_weight, in_sem, send_sem, recv_sem, leave,
):
    mp, tx, ty = (lax.axis_index(a) for a in ("mp", "tx", "ty"))
    n_tx, n_ty = lax.axis_size("tx"), lax.axis_size("ty")
    chip, core = mp // 2, mp % 2
    sib = 1 - core

    def at_chip(by):
        return lax.rem(chip + by + CHIPS, CHIPS)

    def peer(by, other):
        return (at_chip(by) * 2 + (sib if other else core), tx, ty)

    left, right = (mp, jnp.maximum(tx - 1, 0), ty), (mp, jnp.minimum(tx + 1, n_tx - 1), ty)
    before, after = (mp, tx, jnp.maximum(ty - 1, 0)), (mp, tx, jnp.minimum(ty + 1, n_ty - 1))
    has_left, has_right, has_before, has_after = tx > 0, tx < n_tx - 1, ty > 0, ty < n_ty - 1
    greets_left, greeted_right = tx == n_tx - 1, tx == n_tx - 2
    gives_leave = has_left & jnp.logical_not(greets_left)
    needs_leave = has_right & jnp.logical_not(greeted_right)
    peers = [(2, 0), (2, 1), (1, 0), (3, 0), (1, 1), (3, 1), (0, 1)]

    barrier = pltpu.get_barrier_semaphore()

    def greet(device):
        pl.semaphore_signal(barrier, inc=1, device_id=device, device_id_type=MESH)

    for wanted, device in ((has_before, before), (has_after, after), (has_right, right), (greets_left, left)):
        pl.when(wanted)(functools.partial(greet, device))
    for a, b in peers:
        greet(peer(a, b))
    loads = [
        pltpu.make_async_copy(src, dst, in_sem.at[i])
        for i, (src, dst) in enumerate(
            ((x_hbm, tile.at[0]), (d_hbm, tile.at[1]), (coupling_hbm, coupling), (tv_hbm, tv_weight))
        )
    ]
    for load in loads:
        load.start()

    lane = lax.broadcasted_iota(jnp.int32, (NZ, LANES), 1)
    level = lax.broadcasted_iota(jnp.int32, (NZ, LANES), 0)
    inner_z = level < NZ - 1
    zero = jnp.zeros((NZ, LANES), jnp.float32)

    started = []

    def copy(name, src, dst, device):
        i = INDEX[name]
        return pltpu.make_async_remote_copy(
            src_ref=src, dst_ref=dst, send_sem=send_sem.at[i], recv_sem=recv_sem.at[i],
            device_id=device, device_id_type=MESH,
        )

    def send(name, src, device, dst=None, wanted=None):
        c = copy(name, src, src if dst is None else dst, device)
        if wanted is None:
            c.start()
        else:
            pl.when(wanted)(c.start)
        started.append((wanted, c))

    def arrived(name, dst, wanted=None):
        wait = copy(name, dst, dst, peer(0, 1)).wait_recv
        if wanted is None:
            wait()
        else:
            pl.when(wanted)(wait)

    def piece(model, part):
        first, n = {"H": (0, 4), "all": (4, 32)}.get(part) or (4 + 8 * part, 8)
        return held.at[model, pl.ds(first, n)]

    def pack_row(cols, q, r):
        v = held[mp, 2 * ((r + 2) % 18) + q]
        low = pltpu.roll(v, (r + 2) % LANES, 1)
        high = pltpu.roll(v, (r + 97) % LANES, 1)
        cols = jnp.where(lane == r + 1, low, cols)
        return jnp.where(lane == r + 97, high, cols)

    def blank(ref):
        ref[...] = jnp.zeros(ref.shape, jnp.float32)

    rim_after, rim_before = held.at[mp, pl.ds(0, 2)], held.at[mp, pl.ds(2, 2)]
    for missing, ref in (
        (jnp.logical_not(has_after), rim_after), (jnp.logical_not(has_before), rim_before),
        (jnp.logical_not(has_right), got_cols.at[0]), (jnp.logical_not(has_left), got_cols.at[1]),
    ):
        pl.when(missing)(functools.partial(blank, ref))
    for load in loads:
        load.wait()
    for q in range(2):
        for r in range(ROWS):
            held[mp, 2 * (r + 2) + q] = tile[q, pl.ds(r, NZ, stride=ROWS), :]
    for q in range(2):
        cols = zero
        for r in range(ROWS):
            cols = pack_row(cols, q, r)
        own_cols[q] = cols

    expected = len(peers) + sum(w.astype(jnp.int32) for w in (has_before, has_after, has_left, greeted_right))
    pl.semaphore_wait(barrier, expected)

    send("ty0", held.at[mp, pl.ds(4, 2)], before, rim_after, has_before)
    send("ty1", held.at[mp, pl.ds(34, 2)], after, rim_before, has_after)
    for up, down in ((0, 2), (1, 3), (2, 0), (3, 1)):
        send("+O%d" % up, piece(mp, up), peer(1, 0))
        send("-O%d" % down, piece(mp, down), peer(-1, 0))
        if up == 3:
            send("S", piece(mp, "all"), peer(0, 1))

    def give_leave():
        pl.semaphore_signal(leave, inc=1, device_id=left, device_id_type=MESH)

    pl.when(gives_leave)(give_leave)
    def differences(f, f_next, keep_y=None):
        dx = pltpu.roll(f, LANES - 1, 1) - f
        dy = f_next - f
        if keep_y is not None:
            dy = dy * keep_y
        dz = jnp.where(inner_z, pltpu.roll(f, NZ - 1, 0) - f, 0.0)
        return dx, dy, dz

    keep_last = jnp.where(has_after, 1.0, 0.0)

    def row_fields(model, i):
        here = 2 * (i + 1)
        last = isinstance(i, int) and i == ROWS
        then = 0 if last else 2 * (i + 2)
        keep = keep_last if last else None
        g = differences(held[model, here], held[model, then], keep)
        e = differences(held[model, here + 1], held[model, then + 1], keep)
        return g, e

    def add_moments(acc, g, e, weight):
        w = [weight * v for v in g]
        terms = [w[0] * g[0], w[1] * g[1], w[2] * g[2], w[0] * g[1], w[0] * g[2], w[1] * g[2]]
        terms += [e[i] * w[j] for i in range(3) for j in range(3)]
        return terms if acc is None else [a + t for a, t in zip(acc, terms)]

    def row_moments(acc, models, i):
        for model in models:
            g, e = row_fields(model, i)
            acc = add_moments(acc, g, e, coupling[model])
        return acc

    def gather_rows(models, fresh):
        def body(i, carry):
            acc = row_moments(None if fresh else [moms[i, j] for j in range(15)], models, i)
            for j in range(15):
                moms[i, j] = acc[j]
            return carry

        lax.fori_loop(1, ROWS, body, 0, unroll=5)

    prev, nxt, far = at_chip(-1), at_chip(1), at_chip(2)
    pair_own, pair_far = [chip * 2, chip * 2 + 1], [far * 2, far * 2 + 1]

    def relay(d, kind, source, part):
        ref = piece(source * 2 + core, part)
        arrived(d + kind, ref)
        send("X" + d + kind, ref, peer(0, 1))

    def onward(d, kind, source, part):
        send(d + kind, piece(source * 2 + core, part), peer(1 if d == "+" else -1, 0))

    def from_sibling(d, kind, source, part):
        arrived("X" + d + kind, piece(source * 2 + sib, part))

    arrived("ty0", rim_after, has_after)
    arrived("ty1", rim_before, has_before)
    for q in range(2):
        own_cols[q] = pack_row(pack_row(own_cols[q], q, -1), q, ROWS)
    send("tx0", own_cols, left, got_cols.at[0], has_left)
    to_right = copy("tx1", own_cols, got_cols.at[1], right)
    pl.when(greeted_right)(to_right.start)
    started.append((has_right, to_right))
    relay("+", "O0", prev, 0)
    onward("+", "F0", prev, 0)
    relay("-", "O2", nxt, 2)
    onward("-", "F0", nxt, 2)
    relay("+", "O1", prev, 1)
    onward("+", "F1", prev, 1)
    relay("-", "O3", nxt, 3)
    onward("-", "F1", nxt, 3)
    send("+H", piece(mp, "H"), peer(1, 0))
    send("-H", piece(mp, "H"), peer(-1, 0))
    send("2H", piece(mp, "H"), peer(2, 0))
    send("SH", piece(mp, "H"), peer(0, 1))
    arrived("S", piece(chip * 2 + sib, "all"))
    gather_rows(pair_own, True)
    relay("+", "O2", prev, 2)
    relay("-", "O0", nxt, 0)
    relay("+", "O3", prev, 3)
    relay("-", "O1", nxt, 1)
    gather_rows([prev * 2 + core, nxt * 2 + core], False)
    relay("+", "F0", far, 0)
    relay("-", "F0", far, 2)

    def go_right():
        pl.semaphore_wait(leave, 1)
        to_right.start()

    pl.when(needs_leave)(go_right)
    arrived("tx0", got_cols.at[0], has_right)
    arrived("tx1", got_cols.at[1], has_left)
    for q in range(2):
        mine = own_cols[q]
        cols = jnp.where(lane < 64, pltpu.roll(got_cols[1, q], 32, 1), pltpu.roll(got_cols[0, q], 96, 1))
        held[mp, COLS + q] = jnp.where((lane < 32) | (lane >= 96), mine, cols)
    for a, b in peers:
        send("P%d%d" % (a, b), held.at[mp, pl.ds(COLS, 2)], peer(a, b))

    relay("+", "F1", far, 1)
    relay("-", "F1", far, 3)
    relay("+", "H", prev, "H")
    relay("-", "H", nxt, "H")
    relay("2", "H", far, "H")
    for k in range(4):
        from_sibling("+", "O%d" % k, prev, k)
        from_sibling("-", "O%d" % k, nxt, k)
    gather_rows([prev * 2 + sib, nxt * 2 + sib], False)

    alpha = coupling[mp]
    ratio = tv_weight[mp] / alpha

    def fluxes(m, g, e):
        size_sq = g[0] * g[0] + g[1] * g[1] + g[2] * g[2] + EPS_SQ
        tv = ratio * lax.rsqrt(size_sq)
        a00, a11, a22 = m[1] + m[2] + tv, m[0] + m[2] + tv, m[0] + m[1] + tv
        b00, b11, b22 = m[10] + m[14], m[6] + m[14], m[6] + m[10]
        q = (
            a00 * g[0] - (m[3] * g[1] + m[4] * g[2]),
            a11 * g[1] - (m[3] * g[0] + m[5] * g[2]),
            a22 * g[2] - (m[4] * g[0] + m[5] * g[1]),
        )
        p = (
            (a00 * e[0] + b00 * g[0]) - ((m[3] * e[1] + m[4] * e[2]) + (m[7] * g[1] + m[8] * g[2])),
            (a11 * e[1] + b11 * g[1]) - ((m[3] * e[0] + m[5] * e[2]) + (m[9] * g[0] + m[11] * g[2])),
            (a22 * e[2] + b22 * g[2]) - ((m[4] * e[0] + m[5] * e[1]) + (m[12] * g[0] + m[13] * g[1])),
        )
        return q, p

    def along_z(fz):
        fz = jnp.where(inner_z, fz, 0.0)
        return jnp.where(level == 0, 0.0, pltpu.roll(fz, 1, 0)) - fz

    def put_row(i, both, before_y, keep=None):
        new = []
        for q in range(2):
            fx, fy, fz = both[q]
            if keep is not None:
                fy = fy * keep
            enters = jnp.where(lane == 0, 0.0, pltpu.roll(fx, 1, 1))
            rest = jnp.where(lane == LANES - 1, 0.0, before_y[q] - fy + along_z(fz) - fx)
            outs[q, pl.ds(i - 1, NZ, stride=ROWS), :] = alpha * (enters + rest)
            new.append(fy)
        return tuple(new)

    for d, first in (("+", 0), ("-", 2)):
        from_sibling(d, "F0", far, first)
        from_sibling(d, "F1", far, first + 1)

    def out_body(i, carry):
        acc = row_moments([moms[i, j] for j in range(15)], pair_far, i)
        return put_row(i, fluxes(acc, *row_fields(mp, i)), carry)

    carry = lax.fori_loop(1, ROWS, out_body, (zero, zero), unroll=5)

    arrived("SH", piece(chip * 2 + sib, "H"))
    from_sibling("+", "H", prev, "H")
    from_sibling("-", "H", nxt, "H")
    from_sibling("2", "H", far, "H")
    every = range(MODELS)
    put_row(ROWS, fluxes(row_moments(None, every, ROWS), *row_fields(mp, ROWS)), carry, keep_last)
    keep_first = alpha * jnp.where(has_before, 1.0, 0.0)
    entering = [f[1] * keep_first for f in fluxes(row_moments(None, every, 0), *row_fields(mp, 0))]

    for wanted, c in started:
        if wanted is None:
            c.wait_send()
        else:
            pl.when(wanted)(c.wait_send)
    for a, b in peers:
        owner = at_chip(-a) * 2 + (sib if b else core)
        arrived("P%d%d" % (a, b), held.at[owner, pl.ds(COLS, 2)])
    no_x = (lane < 32) & (tx == n_tx - 1)
    no_y = ((lane == ROWS) | (lane == ROWS + 32)) & (ty == n_ty - 1)

    def col_fields(model):
        out = []
        for q in range(2):
            v = held[model, COLS + q]
            dx = jnp.where(no_x, 0.0, pltpu.roll(v, 64, 1) - v)
            dy = jnp.where(no_y, 0.0, pltpu.roll(v, LANES - 1, 1) - v)
            dz = jnp.where(inner_z, pltpu.roll(v, NZ - 1, 0) - v, 0.0)
            out.append((dx, dy, dz))
        return out

    col_moms = None
    for model in range(MODELS):
        g, e = col_fields(model)
        col_moms = add_moments(col_moms, g, e, coupling[model])
    off_x = no_x | ((lane >= 32) & (tx == 0))
    off_y = no_y | ((lane == 0) & (ty == 0))
    for q, f in enumerate(fluxes(col_moms, *col_fields(mp))):
        fx = jnp.where(off_x, 0.0, f[0])
        fy = jnp.where(off_y, 0.0, f[1])
        col_flux[0, q] = alpha * (pltpu.roll(fy, 1, 1) - fy + along_z(f[2]) - fx)
        col_flux[1, q] = alpha * fx
    for q in range(2):
        ends, starts = col_flux[0, q], col_flux[1, q]
        for r in range(ROWS):
            rows = pl.ds(r, NZ, stride=ROWS)
            more = jnp.where(lane == LANES - 1, pltpu.roll(ends, 126 - r, 1), 0.0)
            more = jnp.where(lane == 0, pltpu.roll(starts, 95 - r, 1), more)
            if r == 0:
                more = more + jnp.where(lane == LANES - 1, 0.0, entering[q])
            outs[q, rows, :] = outs[q, rows, :] + more


def shards(models, direction, coupling, tv_weight):
    flat = (NZ * ROWS, LANES)
    n = len(NAMES)
    out = pl.pallas_call(
        kernel,
        name="fused",
        out_shape=pltpu.VMEM((2,) + flat, jnp.float32),
        in_specs=[pl.BlockSpec(memory_space=pl.ANY)] * 4,
        out_specs=pl.BlockSpec(memory_space=pltpu.VMEM),
        scratch_shapes=[
            pltpu.VMEM((MODELS, SLABS, NZ, LANES), jnp.float32),
            pltpu.VMEM((2,) + flat, jnp.float32),
            pltpu.VMEM((ROWS + 1, 15, NZ, LANES), jnp.float32),
            pltpu.VMEM((2, NZ, LANES), jnp.float32),
            pltpu.VMEM((2, 2, NZ, LANES), jnp.float32),
            pltpu.VMEM((2, 2, NZ, LANES), jnp.float32),
            pltpu.SMEM((MODELS,), jnp.float32),
            pltpu.SMEM((MODELS,), jnp.float32),
            pltpu.SemaphoreType.DMA((4,)),
            pltpu.SemaphoreType.DMA((n,)),
            pltpu.SemaphoreType.DMA((n,)),
            pltpu.SemaphoreType.REGULAR,
        ],
        compiler_params=pltpu.CompilerParams(
            collective_id=1, has_side_effects=True, vmem_limit_bytes=60 * 2**20
        ),
    )(models.reshape(flat), direction.reshape(flat), coupling, tv_weight)
    return tuple(out[q].reshape(models.shape) for q in range(2))


def solution(mesh):
    placed = (P("mp", None, "ty", "tx"), P("mp", None, "ty", "tx"), P(), P())
    return jax.shard_map(
        shards,
        mesh=mesh,
        in_specs=placed,
        out_specs=(P("mp", None, "ty", "tx"), P("mp", None, "ty", "tx")),
        check_vma=False,
    )
```

```python
import functools

import jax
import jax.numpy as jnp
from jax import lax
from jax.experimental import pallas as pl
from jax.experimental.pallas import tpu as pltpu
from jax.sharding import PartitionSpec as P

EPS_SQ = 0.25
MESH = pl.DeviceIdType.MESH
MODELS = 8
CHIPS = 4
NZ = 16
ROWS = 16
LANES = 128
SLABS = 38
COLS = 36

RING = ("O0", "O1", "O2", "O3", "H", "F0", "F1")
NAMES = (
    ["ty0", "ty1", "tx0", "tx1", "S", "SH"]
    + [d + k for d in "+-" for k in RING] + ["2H"]
    + ["X" + d + k for d in "+-" for k in RING] + ["X2H"]
    + ["P%d%d" % (a, b) for a in range(CHIPS) for b in range(2) if a + b > 0]
)
INDEX = {name: i for i, name in enumerate(NAMES)}


def kernel(
    x_hbm, d_hbm, coupling_hbm, tv_hbm, outs,
    held, tile, moms, own_cols, got_cols, col_flux, coupling, tv_weight, in_sem, send_sem, recv_sem, leave,
):
    mp, tx, ty = (lax.axis_index(a) for a in ("mp", "tx", "ty"))
    n_tx, n_ty = lax.axis_size("tx"), lax.axis_size("ty")
    chip, core = mp // 2, mp % 2
    sib = 1 - core

    def at_chip(by):
        return lax.rem(chip + by + CHIPS, CHIPS)

    def peer(by, other):
        return (at_chip(by) * 2 + (sib if other else core), tx, ty)

    left, right = (mp, jnp.maximum(tx - 1, 0), ty), (mp, jnp.minimum(tx + 1, n_tx - 1), ty)
    before, after = (mp, tx, jnp.maximum(ty - 1, 0)), (mp, tx, jnp.minimum(ty + 1, n_ty - 1))
    has_left, has_right, has_before, has_after = tx > 0, tx < n_tx - 1, ty > 0, ty < n_ty - 1
    greets_left, greeted_right = tx == n_tx - 1, tx == n_tx - 2
    gives_leave = has_left & jnp.logical_not(greets_left)
    needs_leave = has_right & jnp.logical_not(greeted_right)
    peers = [(2, 0), (2, 1), (1, 0), (3, 0), (1, 1), (3, 1), (0, 1)]

    barrier = pltpu.get_barrier_semaphore()

    def greet(device):
        pl.semaphore_signal(barrier, inc=1, device_id=device, device_id_type=MESH)

    for wanted, device in ((has_before, before), (has_after, after), (has_right, right), (greets_left, left)):
        pl.when(wanted)(functools.partial(greet, device))
    for a, b in peers:
        greet(peer(a, b))
    loads = [
        pltpu.make_async_copy(src, dst, in_sem.at[i])
        for i, (src, dst) in enumerate(
            ((x_hbm, tile.at[0]), (d_hbm, tile.at[1]), (coupling_hbm, coupling), (tv_hbm, tv_weight))
        )
    ]
    for load in loads:
        load.start()

    lane = lax.broadcasted_iota(jnp.int32, (NZ, LANES), 1)
    level = lax.broadcasted_iota(jnp.int32, (NZ, LANES), 0)
    inner_z = level < NZ - 1
    zero = jnp.zeros((NZ, LANES), jnp.float32)

    started = []

    def copy(name, src, dst, device):
        i = INDEX[name]
        return pltpu.make_async_remote_copy(
            src_ref=src, dst_ref=dst, send_sem=send_sem.at[i], recv_sem=recv_sem.at[i],
            device_id=device, device_id_type=MESH,
        )

    def send(name, src, device, dst=None, wanted=None):
        c = copy(name, src, src if dst is None else dst, device)
        if wanted is None:
            c.start()
        else:
            pl.when(wanted)(c.start)
        started.append((wanted, c))

    def arrived(name, dst, wanted=None):
        wait = copy(name, dst, dst, peer(0, 1)).wait_recv
        if wanted is None:
            wait()
        else:
            pl.when(wanted)(wait)

    def piece(model, part):
        first, n = {"H": (0, 4), "all": (4, 32)}.get(part) or (4 + 8 * part, 8)
        return held.at[model, pl.ds(first, n)]

    def pack_row(cols, q, r):
        v = held[mp, 2 * ((r + 2) % 18) + q]
        low = pltpu.roll(v, (r + 2) % LANES, 1)
        high = pltpu.roll(v, (r + 97) % LANES, 1)
        cols = jnp.where(lane == r + 1, low, cols)
        return jnp.where(lane == r + 97, high, cols)

    def blank(ref):
        ref[...] = jnp.zeros(ref.shape, jnp.float32)

    rim_after, rim_before = held.at[mp, pl.ds(0, 2)], held.at[mp, pl.ds(2, 2)]
    for missing, ref in (
        (jnp.logical_not(has_after), rim_after), (jnp.logical_not(has_before), rim_before),
        (jnp.logical_not(has_right), got_cols.at[0]), (jnp.logical_not(has_left), got_cols.at[1]),
    ):
        pl.when(missing)(functools.partial(blank, ref))
    for load in loads:
        load.wait()
    for q in range(2):
        for r in range(ROWS):
            held[mp, 2 * (r + 2) + q] = tile[q, pl.ds(r, NZ, stride=ROWS), :]
    for q in range(2):
        cols = zero
        for r in range(ROWS):
            cols = pack_row(cols, q, r)
        own_cols[q] = cols

    expected = len(peers) + sum(w.astype(jnp.int32) for w in (has_before, has_after, has_left, greeted_right))
    pl.semaphore_wait(barrier, expected)

    send("ty0", held.at[mp, pl.ds(4, 2)], before, rim_after, has_before)
    send("ty1", held.at[mp, pl.ds(34, 2)], after, rim_before, has_after)
    for up, down in ((0, 2), (1, 3), (2, 0), (3, 1)):
        send("+O%d" % up, piece(mp, up), peer(1, 0))
        send("-O%d" % down, piece(mp, down), peer(-1, 0))
        if up == 3:
            send("S", piece(mp, "all"), peer(0, 1))

    def give_leave():
        pl.semaphore_signal(leave, inc=1, device_id=left, device_id_type=MESH)

    pl.when(gives_leave)(give_leave)
    def differences(f, f_next, keep_y=None):
        dx = pltpu.roll(f, LANES - 1, 1) - f
        dy = f_next - f
        if keep_y is not None:
            dy = dy * keep_y
        dz = jnp.where(inner_z, pltpu.roll(f, NZ - 1, 0) - f, 0.0)
        return dx, dy, dz

    keep_last = jnp.where(has_after, 1.0, 0.0)

    def row_fields(model, i):
        here = 2 * (i + 1)
        last = isinstance(i, int) and i == ROWS
        then = 0 if last else 2 * (i + 2)
        keep = keep_last if last else None
        g = differences(held[model, here], held[model, then], keep)
        e = differences(held[model, here + 1], held[model, then + 1], keep)
        return g, e

    def add_moments(acc, g, e, weight):
        w = [weight * v for v in g]
        terms = [w[0] * g[0], w[1] * g[1], w[2] * g[2], w[0] * g[1], w[0] * g[2], w[1] * g[2]]
        terms += [e[i] * w[j] for i in range(3) for j in range(3)]
        return terms if acc is None else [a + t for a, t in zip(acc, terms)]

    def row_moments(acc, models, i):
        for model in models:
            g, e = row_fields(model, i)
            acc = add_moments(acc, g, e, coupling[model])
        return acc

    def gather_rows(models, fresh):
        def body(i, carry):
            acc = row_moments(None if fresh else [moms[i, j] for j in range(15)], models, i)
            for j in range(15):
                moms[i, j] = acc[j]
            return carry

        lax.fori_loop(1, ROWS, body, 0, unroll=5)

    prev, nxt, far = at_chip(-1), at_chip(1), at_chip(2)
    pair_own, pair_far = [chip * 2, chip * 2 + 1], [far * 2, far * 2 + 1]

    def relay(d, kind, source, part, on=None):
        ref = piece(source * 2 + core, part)
        arrived(d + kind, ref)
        if on is not None:
            onward(d, on, source, part)
        send("X" + d + kind, ref, peer(0, 1))

    def onward(d, kind, source, part):
        send(d + kind, piece(source * 2 + core, part), peer(1 if d == "+" else -1, 0))

    def from_sibling(d, kind, source, part):
        arrived("X" + d + kind, piece(source * 2 + sib, part))

    arrived("ty0", rim_after, has_after)
    arrived("ty1", rim_before, has_before)
    for q in range(2):
        own_cols[q] = pack_row(pack_row(own_cols[q], q, -1), q, ROWS)
    send("tx0", own_cols, left, got_cols.at[0], has_left)
    to_right = copy("tx1", own_cols, got_cols.at[1], right)
    pl.when(greeted_right)(to_right.start)
    started.append((has_right, to_right))
    relay("+", "O0", prev, 0, "F0")
    relay("-", "O2", nxt, 2, "F0")
    relay("+", "O1", prev, 1, "F1")
    relay("-", "O3", nxt, 3, "F1")
    send("+H", piece(mp, "H"), peer(1, 0))
    send("-H", piece(mp, "H"), peer(-1, 0))
    send("2H", piece(mp, "H"), peer(2, 0))
    send("SH", piece(mp, "H"), peer(0, 1))
    arrived("S", piece(chip * 2 + sib, "all"))
    gather_rows(pair_own, True)
    relay("+", "O2", prev, 2)
    relay("-", "O0", nxt, 0)
    relay("+", "O3", prev, 3)
    relay("-", "O1", nxt, 1)
    gather_rows([prev * 2 + core, nxt * 2 + core], False)
    relay("+", "F0", far, 0)
    relay("-", "F0", far, 2)

    def go_right():
        pl.semaphore_wait(leave, 1)
        to_right.start()

    pl.when(needs_leave)(go_right)
    arrived("tx0", got_cols.at[0], has_right)
    arrived("tx1", got_cols.at[1], has_left)
    for q in range(2):
        mine = own_cols[q]
        cols = jnp.where(lane < 64, pltpu.roll(got_cols[1, q], 32, 1), pltpu.roll(got_cols[0, q], 96, 1))
        held[mp, COLS + q] = jnp.where((lane < 32) | (lane >= 96), mine, cols)
    for a, b in peers:
        send("P%d%d" % (a, b), held.at[mp, pl.ds(COLS, 2)], peer(a, b))

    relay("+", "F1", far, 1)
    relay("-", "F1", far, 3)
    relay("+", "H", prev, "H")
    relay("-", "H", nxt, "H")
    relay("2", "H", far, "H")
    for k in range(4):
        from_sibling("+", "O%d" % k, prev, k)
        from_sibling("-", "O%d" % k, nxt, k)
    gather_rows([prev * 2 + sib, nxt * 2 + sib], False)

    alpha = coupling[mp]
    ratio = tv_weight[mp] / alpha

    def fluxes(m, g, e):
        size_sq = g[0] * g[0] + g[1] * g[1] + g[2] * g[2] + EPS_SQ
        tv = ratio * lax.rsqrt(size_sq)
        a00, a11, a22 = m[1] + m[2] + tv, m[0] + m[2] + tv, m[0] + m[1] + tv
        b00, b11, b22 = m[10] + m[14], m[6] + m[14], m[6] + m[10]
        q = (
            a00 * g[0] - (m[3] * g[1] + m[4] * g[2]),
            a11 * g[1] - (m[3] * g[0] + m[5] * g[2]),
            a22 * g[2] - (m[4] * g[0] + m[5] * g[1]),
        )
        p = (
            (a00 * e[0] + b00 * g[0]) - ((m[3] * e[1] + m[4] * e[2]) + (m[7] * g[1] + m[8] * g[2])),
            (a11 * e[1] + b11 * g[1]) - ((m[3] * e[0] + m[5] * e[2]) + (m[9] * g[0] + m[11] * g[2])),
            (a22 * e[2] + b22 * g[2]) - ((m[4] * e[0] + m[5] * e[1]) + (m[12] * g[0] + m[13] * g[1])),
        )
        return q, p

    def along_z(fz):
        fz = jnp.where(inner_z, fz, 0.0)
        return jnp.where(level == 0, 0.0, pltpu.roll(fz, 1, 0)) - fz

    def put_row(i, both, before_y, keep=None):
        new = []
        for q in range(2):
            fx, fy, fz = both[q]
            if keep is not None:
                fy = fy * keep
            enters = jnp.where(lane == 0, 0.0, pltpu.roll(fx, 1, 1))
            rest = jnp.where(lane == LANES - 1, 0.0, before_y[q] - fy + along_z(fz) - fx)
            outs[q, pl.ds(i - 1, NZ, stride=ROWS), :] = alpha * (enters + rest)
            new.append(fy)
        return tuple(new)

    for d, first in (("+", 0), ("-", 2)):
        from_sibling(d, "F0", far, first)
        from_sibling(d, "F1", far, first + 1)

    def out_body(i, carry):
        acc = row_moments([moms[i, j] for j in range(15)], pair_far, i)
        return put_row(i, fluxes(acc, *row_fields(mp, i)), carry)

    carry = lax.fori_loop(1, ROWS, out_body, (zero, zero), unroll=5)

    arrived("SH", piece(chip * 2 + sib, "H"))
    from_sibling("+", "H", prev, "H")
    from_sibling("-", "H", nxt, "H")
    from_sibling("2", "H", far, "H")
    every = range(MODELS)
    put_row(ROWS, fluxes(row_moments(None, every, ROWS), *row_fields(mp, ROWS)), carry, keep_last)
    keep_first = alpha * jnp.where(has_before, 1.0, 0.0)
    entering = [f[1] * keep_first for f in fluxes(row_moments(None, every, 0), *row_fields(mp, 0))]

    for wanted, c in started:
        if wanted is None:
            c.wait_send()
        else:
            pl.when(wanted)(c.wait_send)
    for a, b in peers:
        owner = at_chip(-a) * 2 + (sib if b else core)
        arrived("P%d%d" % (a, b), held.at[owner, pl.ds(COLS, 2)])
    no_x = (lane < 32) & (tx == n_tx - 1)
    no_y = ((lane == ROWS) | (lane == ROWS + 32)) & (ty == n_ty - 1)

    def col_fields(model):
        out = []
        for q in range(2):
            v = held[model, COLS + q]
            dx = jnp.where(no_x, 0.0, pltpu.roll(v, 64, 1) - v)
            dy = jnp.where(no_y, 0.0, pltpu.roll(v, LANES - 1, 1) - v)
            dz = jnp.where(inner_z, pltpu.roll(v, NZ - 1, 0) - v, 0.0)
            out.append((dx, dy, dz))
        return out

    col_moms = None
    for model in range(MODELS):
        g, e = col_fields(model)
        col_moms = add_moments(col_moms, g, e, coupling[model])
    off_x = no_x | ((lane >= 32) & (tx == 0))
    off_y = no_y | ((lane == 0) & (ty == 0))
    for q, f in enumerate(fluxes(col_moms, *col_fields(mp))):
        fx = jnp.where(off_x, 0.0, f[0])
        fy = jnp.where(off_y, 0.0, f[1])
        col_flux[0, q] = alpha * (pltpu.roll(fy, 1, 1) - fy + along_z(f[2]) - fx)
        col_flux[1, q] = alpha * fx
    for q in range(2):
        ends, starts = col_flux[0, q], col_flux[1, q]
        for r in range(ROWS):
            rows = pl.ds(r, NZ, stride=ROWS)
            more = jnp.where(lane == LANES - 1, pltpu.roll(ends, 126 - r, 1), 0.0)
            more = jnp.where(lane == 0, pltpu.roll(starts, 95 - r, 1), more)
            if r == 0:
                more = more + jnp.where(lane == LANES - 1, 0.0, entering[q])
            outs[q, rows, :] = outs[q, rows, :] + more


def shards(models, direction, coupling, tv_weight):
    flat = (NZ * ROWS, LANES)
    n = len(NAMES)
    out = pl.pallas_call(
        kernel,
        name="fused",
        out_shape=pltpu.VMEM((2,) + flat, jnp.float32),
        in_specs=[pl.BlockSpec(memory_space=pl.ANY)] * 4,
        out_specs=pl.BlockSpec(memory_space=pltpu.VMEM),
        scratch_shapes=[
            pltpu.VMEM((MODELS, SLABS, NZ, LANES), jnp.float32),
            pltpu.VMEM((2,) + flat, jnp.float32),
            pltpu.VMEM((ROWS + 1, 15, NZ, LANES), jnp.float32),
            pltpu.VMEM((2, NZ, LANES), jnp.float32),
            pltpu.VMEM((2, 2, NZ, LANES), jnp.float32),
            pltpu.VMEM((2, 2, NZ, LANES), jnp.float32),
            pltpu.SMEM((MODELS,), jnp.float32),
            pltpu.SMEM((MODELS,), jnp.float32),
            pltpu.SemaphoreType.DMA((4,)),
            pltpu.SemaphoreType.DMA((n,)),
            pltpu.SemaphoreType.DMA((n,)),
            pltpu.SemaphoreType.REGULAR,
        ],
        compiler_params=pltpu.CompilerParams(
            collective_id=1, has_side_effects=True, vmem_limit_bytes=60 * 2**20
        ),
    )(models.reshape(flat), direction.reshape(flat), coupling, tv_weight)
    return tuple(out[q].reshape(models.shape) for q in range(2))


def solution(mesh):
    placed = (P("mp", None, "ty", "tx"), P("mp", None, "ty", "tx"), P(), P())
    return jax.shard_map(
        shards,
        mesh=mesh,
        in_specs=placed,
        out_specs=(P("mp", None, "ty", "tx"), P("mp", None, "ty", "tx")),
        check_vma=False,
    )
```

```python
import functools

import jax
import jax.numpy as jnp
from jax import lax
from jax.experimental import pallas as pl
from jax.experimental.pallas import tpu as pltpu
from jax.sharding import PartitionSpec as P

EPS_SQ = 0.25
MESH = pl.DeviceIdType.MESH
MODELS = 8
CHIPS = 4
NZ = 16
ROWS = 16
LANES = 128
SLABS = 38
COLS = 36

RING = ("O0", "O1", "O2", "O3", "H", "F0", "F1")
NAMES = (
    ["ty0", "ty1", "tx0", "tx1", "S", "SH"]
    + [d + k for d in "+-" for k in RING] + ["2H"]
    + ["X" + d + k for d in "+-" for k in RING] + ["X2H"]
    + ["P%d%d" % (a, b) for a in range(CHIPS) for b in range(2) if a + b > 0]
)
INDEX = {name: i for i, name in enumerate(NAMES)}


def kernel(
    x_hbm, d_hbm, coupling_hbm, tv_hbm, outs,
    held, tile, moms, own_cols, got_cols, col_flux, coupling, tv_weight, in_sem, send_sem, recv_sem, leave,
):
    mp, tx, ty = (lax.axis_index(a) for a in ("mp", "tx", "ty"))
    n_tx, n_ty = lax.axis_size("tx"), lax.axis_size("ty")
    chip, core = mp // 2, mp % 2
    sib = 1 - core

    def at_chip(by):
        return lax.rem(chip + by + CHIPS, CHIPS)

    def peer(by, other):
        return (at_chip(by) * 2 + (sib if other else core), tx, ty)

    left, right = (mp, jnp.maximum(tx - 1, 0), ty), (mp, jnp.minimum(tx + 1, n_tx - 1), ty)
    before, after = (mp, tx, jnp.maximum(ty - 1, 0)), (mp, tx, jnp.minimum(ty + 1, n_ty - 1))
    has_left, has_right, has_before, has_after = tx > 0, tx < n_tx - 1, ty > 0, ty < n_ty - 1
    greets_left, greeted_right = tx == n_tx - 1, tx == n_tx - 2
    gives_leave = has_left & jnp.logical_not(greets_left)
    needs_leave = has_right & jnp.logical_not(greeted_right)
    peers = [(2, 0), (2, 1), (1, 0), (3, 0), (1, 1), (3, 1), (0, 1)]

    barrier = pltpu.get_barrier_semaphore()

    def greet(device):
        pl.semaphore_signal(barrier, inc=1, device_id=device, device_id_type=MESH)

    for wanted, device in ((has_before, before), (has_after, after), (has_right, right), (greets_left, left)):
        pl.when(wanted)(functools.partial(greet, device))
    for a, b in peers:
        greet(peer(a, b))
    loads = [
        pltpu.make_async_copy(src, dst, in_sem.at[i])
        for i, (src, dst) in enumerate(
            ((x_hbm, tile.at[0]), (d_hbm, tile.at[1]), (coupling_hbm, coupling), (tv_hbm, tv_weight))
        )
    ]
    for load in loads:
        load.start()

    lane = lax.broadcasted_iota(jnp.int32, (NZ, LANES), 1)
    level = lax.broadcasted_iota(jnp.int32, (NZ, LANES), 0)
    inner_z = level < NZ - 1
    zero = jnp.zeros((NZ, LANES), jnp.float32)

    started = []

    def copy(name, src, dst, device):
        i = INDEX[name]
        return pltpu.make_async_remote_copy(
            src_ref=src, dst_ref=dst, send_sem=send_sem.at[i], recv_sem=recv_sem.at[i],
            device_id=device, device_id_type=MESH,
        )

    def send(name, src, device, dst=None, wanted=None):
        c = copy(name, src, src if dst is None else dst, device)
        if wanted is None:
            c.start()
        else:
            pl.when(wanted)(c.start)
        started.append((wanted, c))

    def arrived(name, dst, wanted=None):
        wait = copy(name, dst, dst, peer(0, 1)).wait_recv
        if wanted is None:
            wait()
        else:
            pl.when(wanted)(wait)

    def piece(model, part):
        first, n = {"H": (0, 4), "all": (4, 32)}.get(part) or (4 + 8 * part, 8)
        return held.at[model, pl.ds(first, n)]

    def pack_row(cols, q, r):
        v = held[mp, 2 * ((r + 2) % 18) + q]
        low = pltpu.roll(v, (r + 2) % LANES, 1)
        high = pltpu.roll(v, (r + 97) % LANES, 1)
        cols = jnp.where(lane == r + 1, low, cols)
        return jnp.where(lane == r + 97, high, cols)

    def blank(ref):
        ref[...] = jnp.zeros(ref.shape, jnp.float32)

    rim_after, rim_before = held.at[mp, pl.ds(0, 2)], held.at[mp, pl.ds(2, 2)]
    for missing, ref in (
        (jnp.logical_not(has_after), rim_after), (jnp.logical_not(has_before), rim_before),
        (jnp.logical_not(has_right), got_cols.at[0]), (jnp.logical_not(has_left), got_cols.at[1]),
    ):
        pl.when(missing)(functools.partial(blank, ref))
    for load in loads:
        load.wait()
    for q in range(2):
        for r in range(ROWS):
            held[mp, 2 * (r + 2) + q] = tile[q, pl.ds(r, NZ, stride=ROWS), :]
    for q in range(2):
        cols = zero
        for r in range(ROWS):
            cols = pack_row(cols, q, r)
        own_cols[q] = cols

    expected = len(peers) + sum(w.astype(jnp.int32) for w in (has_before, has_after, has_left, greeted_right))
    pl.semaphore_wait(barrier, expected)

    send("ty0", held.at[mp, pl.ds(4, 2)], before, rim_after, has_before)
    send("ty1", held.at[mp, pl.ds(34, 2)], after, rim_before, has_after)
    for up, down in ((0, 2), (1, 3), (2, 0), (3, 1)):
        send("+O%d" % up, piece(mp, up), peer(1, 0))
        send("-O%d" % down, piece(mp, down), peer(-1, 0))
        if up == 3:
            send("S", piece(mp, "all"), peer(0, 1))

    def give_leave():
        pl.semaphore_signal(leave, inc=1, device_id=left, device_id_type=MESH)

    pl.when(gives_leave)(give_leave)
    def differences(f, f_next, keep_y=None):
        dx = pltpu.roll(f, LANES - 1, 1) - f
        dy = f_next - f
        if keep_y is not None:
            dy = dy * keep_y
        dz = jnp.where(inner_z, pltpu.roll(f, NZ - 1, 0) - f, 0.0)
        return dx, dy, dz

    keep_last = jnp.where(has_after, 1.0, 0.0)

    def row_fields(model, i):
        here = 2 * (i + 1)
        last = isinstance(i, int) and i == ROWS
        then = 0 if last else 2 * (i + 2)
        keep = keep_last if last else None
        g = differences(held[model, here], held[model, then], keep)
        e = differences(held[model, here + 1], held[model, then + 1], keep)
        return g, e

    def add_moments(acc, g, e, weight):
        w = [weight * v for v in g]
        terms = [w[0] * g[0], w[1] * g[1], w[2] * g[2], w[0] * g[1], w[0] * g[2], w[1] * g[2]]
        terms += [e[i] * w[j] for i in range(3) for j in range(3)]
        return terms if acc is None else [a + t for a, t in zip(acc, terms)]

    def row_moments(acc, models, i):
        for model in models:
            g, e = row_fields(model, i)
            acc = add_moments(acc, g, e, coupling[model])
        return acc

    def gather_rows(models, fresh):
        def body(i, carry):
            acc = row_moments(None if fresh else [moms[i, j] for j in range(15)], models, i)
            for j in range(15):
                moms[i, j] = acc[j]
            return carry

        lax.fori_loop(1, ROWS, body, 0, unroll=5)

    prev, nxt, far = at_chip(-1), at_chip(1), at_chip(2)
    pair_own, pair_far = [chip * 2, chip * 2 + 1], [far * 2, far * 2 + 1]

    def relay(d, kind, source, part):
        ref = piece(source * 2 + core, part)
        arrived(d + kind, ref)
        send("X" + d + kind, ref, peer(0, 1))

    def onward(d, kind, source, part):
        send(d + kind, piece(source * 2 + core, part), peer(1 if d == "+" else -1, 0))

    def from_sibling(d, kind, source, part):
        arrived("X" + d + kind, piece(source * 2 + sib, part))

    arrived("ty0", rim_after, has_after)
    arrived("ty1", rim_before, has_before)
    for q in range(2):
        own_cols[q] = pack_row(pack_row(own_cols[q], q, -1), q, ROWS)
    send("tx0", own_cols, left, got_cols.at[0], has_left)
    to_right = copy("tx1", own_cols, got_cols.at[1], right)
    pl.when(greeted_right)(to_right.start)
    started.append((has_right, to_right))
    relay("+", "O0", prev, 0)
    onward("+", "F0", prev, 0)
    relay("-", "O2", nxt, 2)
    onward("-", "F0", nxt, 2)
    relay("+", "O1", prev, 1)
    onward("+", "F1", prev, 1)
    relay("-", "O3", nxt, 3)
    onward("-", "F1", nxt, 3)
    send("2H", piece(mp, "H"), peer(2, 0))
    send("+H", piece(mp, "H"), peer(1, 0))
    send("-H", piece(mp, "H"), peer(-1, 0))
    send("SH", piece(mp, "H"), peer(0, 1))
    arrived("S", piece(chip * 2 + sib, "all"))
    gather_rows(pair_own, True)
    relay("+", "O2", prev, 2)
    relay("-", "O0", nxt, 0)
    relay("+", "O3", prev, 3)
    relay("-", "O1", nxt, 1)
    gather_rows([prev * 2 + core, nxt * 2 + core], False)
    relay("+", "F0", far, 0)
    relay("-", "F0", far, 2)

    def go_right():
        pl.semaphore_wait(leave, 1)
        to_right.start()

    pl.when(needs_leave)(go_right)
    arrived("tx0", got_cols.at[0], has_right)
    arrived("tx1", got_cols.at[1], has_left)
    for q in range(2):
        mine = own_cols[q]
        cols = jnp.where(lane < 64, pltpu.roll(got_cols[1, q], 32, 1), pltpu.roll(got_cols[0, q], 96, 1))
        held[mp, COLS + q] = jnp.where((lane < 32) | (lane >= 96), mine, cols)
    for a, b in peers:
        send("P%d%d" % (a, b), held.at[mp, pl.ds(COLS, 2)], peer(a, b))

    relay("+", "F1", far, 1)
    relay("-", "F1", far, 3)
    relay("+", "H", prev, "H")
    relay("-", "H", nxt, "H")
    relay("2", "H", far, "H")
    for k in range(4):
        from_sibling("+", "O%d" % k, prev, k)
        from_sibling("-", "O%d" % k, nxt, k)
    gather_rows([prev * 2 + sib, nxt * 2 + sib], False)

    alpha = coupling[mp]
    ratio = tv_weight[mp] / alpha

    def fluxes(m, g, e):
        size_sq = g[0] * g[0] + g[1] * g[1] + g[2] * g[2] + EPS_SQ
        tv = ratio * lax.rsqrt(size_sq)
        a00, a11, a22 = m[1] + m[2] + tv, m[0] + m[2] + tv, m[0] + m[1] + tv
        b00, b11, b22 = m[10] + m[14], m[6] + m[14], m[6] + m[10]
        q = (
            a00 * g[0] - (m[3] * g[1] + m[4] * g[2]),
            a11 * g[1] - (m[3] * g[0] + m[5] * g[2]),
            a22 * g[2] - (m[4] * g[0] + m[5] * g[1]),
        )
        p = (
            (a00 * e[0] + b00 * g[0]) - ((m[3] * e[1] + m[4] * e[2]) + (m[7] * g[1] + m[8] * g[2])),
            (a11 * e[1] + b11 * g[1]) - ((m[3] * e[0] + m[5] * e[2]) + (m[9] * g[0] + m[11] * g[2])),
            (a22 * e[2] + b22 * g[2]) - ((m[4] * e[0] + m[5] * e[1]) + (m[12] * g[0] + m[13] * g[1])),
        )
        return q, p

    def along_z(fz):
        fz = jnp.where(inner_z, fz, 0.0)
        return jnp.where(level == 0, 0.0, pltpu.roll(fz, 1, 0)) - fz

    def put_row(i, both, before_y, keep=None):
        new = []
        for q in range(2):
            fx, fy, fz = both[q]
            if keep is not None:
                fy = fy * keep
            enters = jnp.where(lane == 0, 0.0, pltpu.roll(fx, 1, 1))
            rest = jnp.where(lane == LANES - 1, 0.0, before_y[q] - fy + along_z(fz) - fx)
            outs[q, pl.ds(i - 1, NZ, stride=ROWS), :] = alpha * (enters + rest)
            new.append(fy)
        return tuple(new)

    for d, first in (("+", 0), ("-", 2)):
        from_sibling(d, "F0", far, first)
        from_sibling(d, "F1", far, first + 1)

    def out_body(i, carry):
        acc = row_moments([moms[i, j] for j in range(15)], pair_far, i)
        return put_row(i, fluxes(acc, *row_fields(mp, i)), carry)

    carry = lax.fori_loop(1, ROWS, out_body, (zero, zero), unroll=5)

    arrived("SH", piece(chip * 2 + sib, "H"))
    from_sibling("+", "H", prev, "H")
    from_sibling("-", "H", nxt, "H")
    from_sibling("2", "H", far, "H")
    every = range(MODELS)
    put_row(ROWS, fluxes(row_moments(None, every, ROWS), *row_fields(mp, ROWS)), carry, keep_last)
    keep_first = alpha * jnp.where(has_before, 1.0, 0.0)
    entering = [f[1] * keep_first for f in fluxes(row_moments(None, every, 0), *row_fields(mp, 0))]

    for wanted, c in started:
        if wanted is None:
            c.wait_send()
        else:
            pl.when(wanted)(c.wait_send)
    for a, b in peers:
        owner = at_chip(-a) * 2 + (sib if b else core)
        arrived("P%d%d" % (a, b), held.at[owner, pl.ds(COLS, 2)])
    no_x = (lane < 32) & (tx == n_tx - 1)
    no_y = ((lane == ROWS) | (lane == ROWS + 32)) & (ty == n_ty - 1)

    def col_fields(model):
        out = []
        for q in range(2):
            v = held[model, COLS + q]
            dx = jnp.where(no_x, 0.0, pltpu.roll(v, 64, 1) - v)
            dy = jnp.where(no_y, 0.0, pltpu.roll(v, LANES - 1, 1) - v)
            dz = jnp.where(inner_z, pltpu.roll(v, NZ - 1, 0) - v, 0.0)
            out.append((dx, dy, dz))
        return out

    col_moms = None
    for model in range(MODELS):
        g, e = col_fields(model)
        col_moms = add_moments(col_moms, g, e, coupling[model])
    off_x = no_x | ((lane >= 32) & (tx == 0))
    off_y = no_y | ((lane == 0) & (ty == 0))
    for q, f in enumerate(fluxes(col_moms, *col_fields(mp))):
        fx = jnp.where(off_x, 0.0, f[0])
        fy = jnp.where(off_y, 0.0, f[1])
        col_flux[0, q] = alpha * (pltpu.roll(fy, 1, 1) - fy + along_z(f[2]) - fx)
        col_flux[1, q] = alpha * fx
    for q in range(2):
        ends, starts = col_flux[0, q], col_flux[1, q]
        for r in range(ROWS):
            rows = pl.ds(r, NZ, stride=ROWS)
            more = jnp.where(lane == LANES - 1, pltpu.roll(ends, 126 - r, 1), 0.0)
            more = jnp.where(lane == 0, pltpu.roll(starts, 95 - r, 1), more)
            if r == 0:
                more = more + jnp.where(lane == LANES - 1, 0.0, entering[q])
            outs[q, rows, :] = outs[q, rows, :] + more


def shards(models, direction, coupling, tv_weight):
    flat = (NZ * ROWS, LANES)
    n = len(NAMES)
    out = pl.pallas_call(
        kernel,
        name="fused",
        out_shape=pltpu.VMEM((2,) + flat, jnp.float32),
        in_specs=[pl.BlockSpec(memory_space=pl.ANY)] * 4,
        out_specs=pl.BlockSpec(memory_space=pltpu.VMEM),
        scratch_shapes=[
            pltpu.VMEM((MODELS, SLABS, NZ, LANES), jnp.float32),
            pltpu.VMEM((2,) + flat, jnp.float32),
            pltpu.VMEM((ROWS + 1, 15, NZ, LANES), jnp.float32),
            pltpu.VMEM((2, NZ, LANES), jnp.float32),
            pltpu.VMEM((2, 2, NZ, LANES), jnp.float32),
            pltpu.VMEM((2, 2, NZ, LANES), jnp.float32),
            pltpu.SMEM((MODELS,), jnp.float32),
            pltpu.SMEM((MODELS,), jnp.float32),
            pltpu.SemaphoreType.DMA((4,)),
            pltpu.SemaphoreType.DMA((n,)),
            pltpu.SemaphoreType.DMA((n,)),
            pltpu.SemaphoreType.REGULAR,
        ],
        compiler_params=pltpu.CompilerParams(
            collective_id=1, has_side_effects=True, vmem_limit_bytes=60 * 2**20
        ),
    )(models.reshape(flat), direction.reshape(flat), coupling, tv_weight)
    return tuple(out[q].reshape(models.shape) for q in range(2))


def solution(mesh):
    placed = (P("mp", None, "ty", "tx"), P("mp", None, "ty", "tx"), P(), P())
    return jax.shard_map(
        shards,
        mesh=mesh,
        in_specs=placed,
        out_specs=(P("mp", None, "ty", "tx"), P("mp", None, "ty", "tx")),
        check_vma=False,
    )
```
